32 devices in a mesh: seq: 8 (over z, core), section: 2 (over y), tp: 2 (over x).
Axes of the slice: x: 2, y: 2, z: 4, core: 2. Of those that a mesh axis runs over, the one named last changes fastest.
Arguments:
- h_in: bfloat16 [2, 2048, 3072], P('section', 'seq', 'tp'), may hold values from -32 to 32
- memory: bfloat16 [2, 2048, 3072], P('section', 'seq', 'tp'), may hold values from -32 to 32
- cotangent: bfloat16 [2, 2048, 3072], P('section', 'seq', 'tp'), may hold values from -6 to 6
- block_docs: int32 [2, 16], P('section', 'seq'), may hold values from 0 to 3, never falling along the last dimension, each value on 1 to 12 neighbouring positions
- w_query: bfloat16 [2, 3072, 1536], P('section', None, 'tp'), may hold values from -0.109375 to 0.109375
- w_out: bfloat16 [2, 1536, 3072], P('section', 'tp'), may hold values from -0.15625 to 0.15625
- self_key_value_weight: bfloat16 [3072, 2, 512], P(None, None, 'tp'), may hold values from -0.109375 to 0.109375
- cache_key_value_weight: bfloat16 [3072, 2, 512], P(None, None, 'tp'), may hold values from -0.109375 to 0.109375
Outputs:
- passed_forward: bfloat16 [2, 2048, 3072], P('section', 'seq', 'tp')
- grad_input: bfloat16 [2, 2048, 3072], P('section', 'seq', 'tp')
- grad_memory: bfloat16 [2, 2048, 3072], P('section', 'seq', 'tp')
- grad_w_query: float32 [2, 3072, 1536], P('section', 'seq', 'tp')
- grad_w_out: float32 [2, 1536, 3072], P('section', 'tp', 'seq')
- grad_w_self_kv: float32 [3072, 2, 512], P(('seq', 'section'), None, 'tp')
- grad_w_cache: float32 [3072, 2, 512], P(('seq', 'section'), None, 'tp')
The draws below stay inside these ranges and needn't reach their ends.
Inputs may be any that keep to these rules, and one draw needn't show every extreme that they name: block_docs[s, b] is the document of tokens b * 128 to b * 128 + 127 of section s; numbers never fall along a row, and in every row one document spans exactly 12 blocks.
All inputs are finite; a program needn't handle non-finite values.
Results may differ from the reference program's by a relative error of at most 0.02.
Values may be sent and summed in bfloat16 or wider, within the bound.
No kernel may reach another device: no remote copies, remote signals or barrier semaphores. Data moves between devices by JAX's collectives and lax.ppermute only.
A program may use at most 128 MiB of HBM per device.

```python
import math
import jax
import jax.numpy as jnp
import numpy as np
from jax import lax

MODEL_DIM = 3072
QUERY_HEAD_COUNT = 12
KEY_VALUE_HEADS = 4
HEAD_DIM = 128
BLK = 128
WIN = 1024
DOCS = 4
SEQ = 2048
NBLK = 16
N_SECTION = 2
N_TP = 2


def draw_hidden_states(key, salt):
    base_key = jax.random.fold_in(key, salt)
    noise_key, row_key = jax.random.split(base_key)
    shape = (N_SECTION, SEQ, MODEL_DIM)
    place = jnp.arange(MODEL_DIM, dtype=jnp.float32) / max(MODEL_DIM - 1, 1)
    noise = jnp.clip(jax.random.normal(noise_key, shape, jnp.float32), -6.0, 6.0)
    feature_scale = jnp.exp(math.log(10.0) * place) / 4.0
    row_scale = jnp.exp(jax.random.uniform(row_key, (N_SECTION, SEQ, 1), jnp.float32, math.log(0.5), math.log(2.0)))
    return (noise * feature_scale[None, None, :] * row_scale).astype(jnp.bfloat16)


def draw_h_in(key, part):
    return draw_hidden_states(key, 11)


def draw_memory(key, part):
    return draw_hidden_states(key, 23)


def level_of(rng, extent, shards, smallest, largest):
    factor_of, own = 1.0, jax.random.fold_in(rng, 6)
    for position, parts in shards:
        heights = jnp.exp(jax.random.uniform(jax.random.fold_in(own, position), (parts,), jnp.float32, smallest / len(shards), largest / len(shards)))
        factor_of = factor_of * jnp.repeat(heights, extent[position] // parts).reshape([-1 if axis == position else 1 for axis in range(len(extent))])
    return factor_of


def length_profile(amount, total, limit, slope):
    loads = [(1 << 20) // math.isqrt(rank ** slope) + 1 for rank in range(2, amount + 1)]
    surplus, counts = total - limit - (amount - 1), [1] * (amount - 1)
    while surplus > 0:
        movable = [i for i in range(amount - 1) if counts[i] < limit]
        mass, remaining = sum([loads[i] for i in movable]), surplus
        for i in movable:
            addition = min(limit - counts[i], max(1, remaining * loads[i] // mass), surplus)
            counts[i] = counts[i] + addition
            surplus = surplus - addition
    return np.array([limit] + counts)


def ragged(own_key, number_of, total, limit, lean):
    if number_of == 2:
        one = jax.random.randint(own_key, (), max(1, total - limit), min(limit, total - 1) + 1)
        return jnp.stack([one, total - one])
    lengths = jnp.asarray(length_profile(number_of, total, limit, lean), jnp.int32)
    pairs = (number_of - 1) // 2
    giver, receiver = lengths[1:1 + 2 * pairs:2], lengths[2:2 + 2 * pairs:2]
    slack = jnp.minimum(giver - 1, limit - receiver)
    moved = jax.random.randint(jax.random.fold_in(own_key, 1), (pairs,), 0, 1 << 20) % (slack + 1)
    lengths = lengths.at[1:1 + 2 * pairs:2].set(giver - moved).at[2:2 + 2 * pairs:2].set(receiver + moved)
    return lengths[jax.random.permutation(jax.random.fold_in(own_key, 2), number_of)]


def centred(own_key, extent, width, limit, pieces=(), kind=jnp.bfloat16):
    values = jax.random.normal(own_key, extent, jnp.float32) * width
    if len(pieces) > 0:
        values = level_of(own_key, extent, pieces, -0.22, 0.18) * values
    return jnp.clip(values, min=-limit, max=limit).astype(kind)


def setup_inputs(seed: int = 0) -> dict:
    streams_of = jax.random.split(jax.random.key(seed), 9)
    return {
        "h_in": draw_h_in(jax.random.fold_in(streams_of[8], 71), 0),
        "memory": draw_memory(jax.random.fold_in(streams_of[8], 71), 0),
        "cotangent": centred(streams_of[2], (N_SECTION, SEQ, MODEL_DIM), 1.0, 6.0, ((0, 2), (1, 8), (2, 2))),
        "block_docs": jax.vmap(lambda own: jnp.searchsorted(jnp.cumsum(ragged(own, DOCS, NBLK, 3 * NBLK // 4, 1)), jnp.arange(NBLK), side="right"))(jax.random.split(streams_of[3], N_SECTION)).reshape((N_SECTION, NBLK)).astype(jnp.int32),
        "w_query": centred(streams_of[4], (N_SECTION, MODEL_DIM, QUERY_HEAD_COUNT * HEAD_DIM), MODEL_DIM ** -0.5, 0.109375, ((0, 2), (2, 2))),
        "w_out": centred(streams_of[5], (N_SECTION, QUERY_HEAD_COUNT * HEAD_DIM, MODEL_DIM), (QUERY_HEAD_COUNT * HEAD_DIM) ** -0.5, 0.15625, ((0, 2), (1, 2))),
        "self_key_value_weight": centred(streams_of[6], (MODEL_DIM, 2, KEY_VALUE_HEADS * HEAD_DIM), MODEL_DIM ** -0.5, 0.109375, ((2, 2),)),
        "cache_key_value_weight": centred(streams_of[7], (MODEL_DIM, 2, KEY_VALUE_HEADS * HEAD_DIM), MODEL_DIM ** -0.5, 0.109375, ((2, 2),)),
    }


score_scale = 40.0
norm_eps = 1e-06

def to_rounded(values):
    return lax.optimization_barrier(values.astype(jnp.bfloat16)).astype(jnp.float32)

def row_norm(values):
    wide_vals = values.astype(jnp.float32)
    factor = lax.rsqrt(lax.optimization_barrier(jnp.mean(wide_vals * wide_vals, axis=-1)) + norm_eps)
    return ((wide_vals * factor[:, None]).astype(jnp.bfloat16), factor)

def unit_rows(values):
    return values * lax.rsqrt(lax.optimization_barrier(jnp.sum(values * values, axis=-1, keepdims=True)) + norm_eps)

def visible(query_pos, query_doc, key_pos, key_doc, self_section):
    upper_bound = jnp.where(self_section, query_pos, query_pos // BLK * BLK + BLK - 1)
    lower_bound = jnp.where(self_section, query_pos - WIN, -1)
    same_doc = query_doc[:, None] == key_doc[None, :]
    return same_doc & (key_pos[None, :] <= upper_bound[:, None]) & (key_pos[None, :] > lower_bound[:, None])

def section_pass(self_section, hidden, source, grad_out, docs, query_projection_weight, out_weight, key_value_matrix):
    sequence_length_total = hidden.shape[0]
    hidden_model_width = hidden.shape[1]
    query_group_width = QUERY_HEAD_COUNT // KEY_VALUE_HEADS
    normalized_input, row_factor = row_norm(hidden)
    normalized_source, source_factor = row_norm(source)
    key_value_flattened = key_value_matrix.reshape(hidden_model_width, 2 * KEY_VALUE_HEADS * HEAD_DIM)
    query_matrix = jnp.dot(normalized_input, query_projection_weight, preferred_element_type=jnp.float32).reshape(sequence_length_total, KEY_VALUE_HEADS, query_group_width, HEAD_DIM)
    key_value_pairs = jnp.dot(normalized_source, key_value_flattened, preferred_element_type=jnp.float32).reshape(sequence_length_total, 2, KEY_VALUE_HEADS, HEAD_DIM)
    query_unit = unit_rows(query_matrix).astype(jnp.bfloat16)
    key_raw = key_value_pairs[:, 0]
    key_unit = unit_rows(key_raw).astype(jnp.bfloat16)
    value_bf = key_value_pairs[:, 1].astype(jnp.bfloat16)
    key_wide = key_unit.astype(jnp.float32)
    value_wide = value_bf.astype(jnp.float32)
    positions = jnp.arange(sequence_length_total, dtype=jnp.int32)
    doc_of = jnp.repeat(docs, BLK)
    span_len = math.gcd(sequence_length_total, 512)
    block_count = sequence_length_total // span_len

    def block_rows(values, block_index):
        return lax.dynamic_slice_in_dim(values, (block_index * span_len).astype(jnp.int32), span_len, 0)

    def block_scores(block_index):
        query_block = block_rows(query_unit, block_index).astype(jnp.float32)
        allowed = visible(block_rows(positions, block_index), block_rows(doc_of, block_index), positions, doc_of, self_section)
        scores = score_scale * jnp.einsum('tgjd,ugd->tgju', query_block, key_wide)
        return (query_block, allowed[:, None, None, :], scores)

    def forward_block(block_index):
        query_block, allowed, scores = block_scores(block_index)
        weights = jnp.where(allowed, jnp.exp(scores), 0.0)
        softmax_denominator = lax.optimization_barrier(jnp.sum(weights, axis=-1))
        numerator = jnp.einsum('tgju,ugd->tgjd', to_rounded(weights), value_wide)
        return (numerator / softmax_denominator[..., None], softmax_denominator)
    block_outputs, denominator_rows = lax.map(forward_block, jnp.arange(block_count, dtype=jnp.int32))
    attention_output = block_outputs.reshape(sequence_length_total, KEY_VALUE_HEADS, query_group_width, HEAD_DIM).astype(jnp.bfloat16)
    softmax_denominator = denominator_rows.reshape(sequence_length_total, KEY_VALUE_HEADS, query_group_width)
    attn_flat = attention_output.reshape(sequence_length_total, QUERY_HEAD_COUNT * HEAD_DIM)
    projected = jnp.dot(attn_flat, out_weight, preferred_element_type=jnp.float32)
    h_out = (hidden.astype(jnp.float32) + projected).astype(jnp.bfloat16)
    attention_gradient = lax.dot_general(grad_out, out_weight, (((1,), (1,)), ((), ())), preferred_element_type=jnp.float32)
    attention_gradient = attention_gradient.astype(jnp.bfloat16).reshape(sequence_length_total, KEY_VALUE_HEADS, query_group_width, HEAD_DIM)
    grad_attn_wide = attention_gradient.astype(jnp.float32)
    delta = lax.optimization_barrier(jnp.sum(grad_attn_wide * attention_output.astype(jnp.float32), axis=-1))

    def backward_block(running, block_index):
        grad_key, value_gradient = running
        query_block, allowed, scores = block_scores(block_index)
        grad_block = block_rows(grad_attn_wide, block_index)
        probs = jnp.where(allowed, jnp.exp(scores) / block_rows(softmax_denominator, block_index)[..., None], 0.0)
        grad_probs = jnp.einsum('tgjd,ugd->tgju', grad_block, value_wide)
        grad_scores = to_rounded(probs * (grad_probs - block_rows(delta, block_index)[..., None]))
        query_gradient = score_scale * jnp.einsum('tgju,ugd->tgjd', grad_scores, key_wide)
        grad_key = grad_key + score_scale * jnp.einsum('tgju,tgjd->ugd', grad_scores, query_block)
        value_gradient = value_gradient + jnp.einsum('tgju,tgjd->ugd', to_rounded(probs), grad_block)
        return ((grad_key, value_gradient), query_gradient)
    empty_gradients = jnp.zeros((sequence_length_total, KEY_VALUE_HEADS, HEAD_DIM), jnp.float32)
    (grad_key, value_gradient), query_gradient = lax.scan(backward_block, (empty_gradients, empty_gradients), jnp.arange(block_count, dtype=jnp.int32))
    query_gradient = query_gradient.reshape(sequence_length_total, KEY_VALUE_HEADS, query_group_width, HEAD_DIM)
    _, query_pull = jax.vjp(unit_rows, query_matrix)
    grad_queries = query_pull(query_gradient)[0].reshape(sequence_length_total, QUERY_HEAD_COUNT * HEAD_DIM).astype(jnp.bfloat16)
    _, key_pull = jax.vjp(unit_rows, key_raw)
    key_gradient_rows = key_pull(grad_key)[0]
    key_value_gradient = jnp.stack([key_gradient_rows, value_gradient], axis=1).reshape(sequence_length_total, 2, KEY_VALUE_HEADS * HEAD_DIM).astype(jnp.bfloat16)
    query_cols = QUERY_HEAD_COUNT * HEAD_DIM // N_TP
    key_value_columns = KEY_VALUE_HEADS * HEAD_DIM // N_TP
    back_rows = jnp.zeros((sequence_length_total, hidden_model_width), jnp.float32)
    back_source = jnp.zeros((sequence_length_total, hidden_model_width), jnp.float32)
    for tp_part in range(N_TP):
        query_first = tp_part * query_cols
        kv_first = tp_part * key_value_columns
        product = lax.dot_general(grad_queries[:, query_first:query_first + query_cols], query_projection_weight[:, query_first:query_first + query_cols], (((1,), (1,)), ((), ())), preferred_element_type=jnp.float32)
        back_rows = back_rows + to_rounded(product)
        grad_part = key_value_gradient[:, :, kv_first:kv_first + key_value_columns].reshape(sequence_length_total, 2 * key_value_columns)
        weight_part = key_value_matrix[:, :, kv_first:kv_first + key_value_columns].reshape(hidden_model_width, 2 * key_value_columns)
        product = lax.dot_general(grad_part, weight_part, (((1,), (1,)), ((), ())), preferred_element_type=jnp.float32)
        back_source = back_source + to_rounded(product)
    hidden_wide = hidden.astype(jnp.float32)
    source_wide = source.astype(jnp.float32)
    row_total = lax.optimization_barrier(jnp.sum(back_rows * hidden_wide, axis=1))
    source_total = lax.optimization_barrier(jnp.sum(back_source * source_wide, axis=1))
    row_cube = row_factor * row_factor * row_factor
    source_cube = source_factor * source_factor * source_factor
    grad_input = grad_out.astype(jnp.float32) + row_factor[:, None] * back_rows - hidden_wide * (row_cube * row_total / hidden_model_width)[:, None]
    grad_memory = source_factor[:, None] * back_source - source_wide * (source_cube * source_total / hidden_model_width)[:, None]
    grad_wq = lax.dot_general(normalized_input, grad_queries, (((0,), (0,)), ((), ())), preferred_element_type=jnp.float32)
    grad_wo = lax.dot_general(attn_flat, grad_out, (((0,), (0,)), ((), ())), preferred_element_type=jnp.float32)
    key_value_weight_gradient = lax.dot_general(normalized_source, key_value_gradient.reshape(sequence_length_total, 2 * KEY_VALUE_HEADS * HEAD_DIM), (((0,), (0,)), ((), ())), preferred_element_type=jnp.float32)
    key_value_weight_gradient = key_value_weight_gradient.reshape(hidden_model_width, 2, KEY_VALUE_HEADS * HEAD_DIM)
    return (h_out, grad_input.astype(jnp.bfloat16), grad_memory.astype(jnp.bfloat16), grad_wq, grad_wo, key_value_weight_gradient)

def reference(h_in, memory, cotangent, block_docs, w_query, w_out, self_key_value_weight, cache_key_value_weight):
    results = []
    for section_id in range(N_SECTION):
        if section_id == 0:
            source = h_in[0]
            key_value_matrix = self_key_value_weight
        else:
            source = memory[section_id]
            key_value_matrix = cache_key_value_weight
        results.append(section_pass(section_id == 0, h_in[section_id], source, cotangent[section_id], block_docs[section_id], w_query[section_id], w_out[section_id], key_value_matrix))
    outputs = jnp.stack([entry[0] for entry in results])
    passed_forward = jnp.roll(outputs, 1, axis=0)
    grad_input = jnp.stack([entry[1] for entry in results])
    grad_memory = jnp.stack([entry[2] for entry in results])
    grad_w_query = jnp.stack([entry[3] for entry in results])
    grad_w_out = jnp.stack([entry[4] for entry in results])
    grad_w_self_kv = results[0][5]
    grad_w_cache = results[1][5]
    for section_id in range(2, N_SECTION):
        grad_w_cache = grad_w_cache + results[section_id][5]
    return (passed_forward, grad_input, grad_memory, grad_w_query, grad_w_out, grad_w_self_kv, grad_w_cache)
```

```python
import functools

import jax
import jax.numpy as jnp
from jax import lax
from jax.experimental import pallas as pl
from jax.experimental.pallas import tpu as pltpu
from jax.sharding import PartitionSpec as P

HEAD_DIM = 128
BLK = 128
WIN = 1024

score_scale = 40.0
norm_eps = 1e-06

F32 = jnp.float32
BF16 = jnp.bfloat16
NN = (((1,), (0,)), ((), ()))
NT = (((1,), (1,)), ((), ()))
TN = (((0,), (0,)), ((), ()))

VMEM = pl.BlockSpec(memory_space=pltpu.VMEM)
SMEM = pl.BlockSpec(memory_space=pltpu.SMEM)


def dot(left, right, dims):
    return lax.dot_general(left, right, dims, preferred_element_type=F32)


def shifted(value, axis, steps):
    count = lax.axis_size(axis)
    pairs = [(source, (source + steps) % count) for source in range(count)]
    return lax.ppermute(value, axis, pairs)


def call(body, out_shape, inputs, smem_count, flops, scratch=(), limit=40):
    moved = sum(v.size * v.dtype.itemsize for v in inputs) + sum(
        o.size * o.dtype.itemsize for o in out_shape
    )
    return pl.pallas_call(
        body,
        out_shape=out_shape,
        in_specs=[SMEM] * smem_count + [VMEM] * (len(inputs) - smem_count),
        out_specs=[VMEM] * len(out_shape),
        scratch_shapes=list(scratch),
        compiler_params=pltpu.CompilerParams(vmem_limit_bytes=limit * 1024 * 1024),
        cost_estimate=pl.CostEstimate(flops=flops, bytes_accessed=moved, transcendentals=0),
    )(*inputs)


def struct(shape, dtype):
    return jax.ShapeDtypeStruct(shape, dtype)


def offset(me, count, step, width):
    return pl.multiple_of(lax.rem(me + count - step, count) * width, width)


def normalize(pieces, me, normed_ref, factor_ref):
    count = len(pieces)
    width = pieces[0].shape[1]
    total = 0.0
    for piece in pieces:
        wide = piece[...].astype(F32)
        total = total + jnp.sum(wide * wide, axis=1, keepdims=True)
    factor = lax.rsqrt(total / (count * width) + norm_eps)
    factor_ref[...] = jnp.broadcast_to(factor, factor_ref.shape)
    for step, piece in enumerate(pieces):
        normed_ref[:, pl.ds(offset(me, count, step, width), width)] = (
            piece[...].astype(F32) * factor
        ).astype(BF16)


def unit(raw):
    return raw * lax.rsqrt(jnp.sum(raw * raw, axis=1, keepdims=True) + norm_eps)


def unit_back(raw, grad):
    scale = lax.rsqrt(jnp.sum(raw * raw, axis=1, keepdims=True) + norm_eps)
    along = jnp.sum(raw * grad, axis=1, keepdims=True)
    return scale * grad - raw * (scale * scale * scale * along)


def query_body(count, me_ref, *refs):
    pieces, (weight, normed_ref, factor_ref, unit_ref, raw_ref) = refs[:count], refs[count:]
    normalize(pieces, me_ref[0], normed_ref, factor_ref)
    for head in range(unit_ref.shape[0]):
        cols = slice(head * HEAD_DIM, (head + 1) * HEAD_DIM)
        if head % 2 == 0:
            last = min(head + 2, unit_ref.shape[0]) * HEAD_DIM
            pair = dot(normed_ref[...], weight[:, head * HEAD_DIM : last], NN)
        raw = pair[:, (head % 2) * HEAD_DIM : (head % 2 + 1) * HEAD_DIM]
        raw_ref[head] = raw
        unit_ref[head] = unit(raw).astype(BF16)


def key_body(count, me_ref, *refs):
    pieces, (weight, normed_ref, factor_ref, packed_ref, raw_ref) = refs[:count], refs[count:]
    normalize(pieces, me_ref[0], normed_ref, factor_ref)
    both = dot(normed_ref[...], weight[...], NN)
    half = both.shape[1] // 2
    for head in range(half // HEAD_DIM):
        cols = slice(head * HEAD_DIM, (head + 1) * HEAD_DIM)
        packed_ref[:, cols] = unit(both[:, cols]).astype(BF16)
    packed_ref[:, half:] = both[:, half:].astype(BF16)
    raw_ref[...] = both[:, :half]


def allowed_block(meta, block, rows):
    per = rows // BLK
    shard, self_section = meta[0], meta[1]
    shape = (rows, rows)
    row = lax.broadcasted_iota(jnp.int32, shape, 0)
    col = lax.broadcasted_iota(jnp.int32, shape, 1)
    query_doc = jnp.full(shape, meta[3 + shard * per], jnp.int32)
    key_doc = jnp.full(shape, meta[3 + block * per], jnp.int32)
    for part in range(1, per):
        query_doc = jnp.where(row >= part * BLK, meta[3 + shard * per + part], query_doc)
        key_doc = jnp.where(col >= part * BLK, meta[3 + block * per + part], key_doc)
    query_pos = shard * rows + row
    key_pos = block * rows + col
    is_self = jnp.full(shape, self_section, jnp.int32) == 1
    upper = jnp.where(is_self, query_pos, query_pos // BLK * BLK + BLK - 1)
    lower = jnp.where(is_self, query_pos - WIN, -1)
    return (query_doc == key_doc) & (key_pos <= upper) & (key_pos > lower)


def forward_body(kv_heads, meta, query_ref, kv_ref, out_ref, inverse_ref, number_ref, denom_ref):
    heads, rows, _ = query_ref.shape
    group = heads // kv_heads
    number_ref[...] = jnp.zeros_like(number_ref)
    denom_ref[...] = jnp.zeros_like(denom_ref)

    def step(block, carry):
        allowed = allowed_block(meta, block, rows)
        span = pl.ds(pl.multiple_of(block * rows, rows), rows)
        for kv_head in range(kv_heads):
            key = kv_ref[span, kv_head * HEAD_DIM : (kv_head + 1) * HEAD_DIM]
            first = (kv_heads + kv_head) * HEAD_DIM
            value = kv_ref[span, first : first + HEAD_DIM]
            for head in range(kv_head * group, (kv_head + 1) * group):
                score = dot(query_ref[head], key, NT)
                weight = jnp.where(allowed, jnp.exp(score_scale * score), 0.0)
                folded = weight[:, :HEAD_DIM]
                for part in range(1, rows // HEAD_DIM):
                    folded = folded + weight[:, part * HEAD_DIM : (part + 1) * HEAD_DIM]
                denom_ref[head] += folded
                number_ref[head] += dot(weight.astype(BF16), value, NN)
        return carry

    lax.fori_loop(meta[2], meta[0] + 1, step, 0)
    for head in range(heads):
        inverse = 1.0 / jnp.sum(denom_ref[head], axis=1, keepdims=True)
        inverse_ref[head] = jnp.broadcast_to(inverse, (rows, HEAD_DIM))
        out_ref[:, head * HEAD_DIM : (head + 1) * HEAD_DIM] = (number_ref[head] * inverse).astype(BF16)


def grad_attn_body(count, me_ref, *refs):
    pieces, (weight, full_ref, grad_ref) = refs[:count], refs[count:]
    width = pieces[0].shape[1]
    for step, piece in enumerate(pieces):
        full_ref[:, pl.ds(offset(me_ref[0], count, step, width), width)] = piece[...]
    for head in range(grad_ref.shape[0]):
        if head % 2 == 0:
            last = min(head + 2, grad_ref.shape[0]) * HEAD_DIM
            pair = dot(full_ref[...], weight[head * HEAD_DIM : last, :], NT)
        grad_ref[head] = pair[:, (head % 2) * HEAD_DIM : (head % 2 + 1) * HEAD_DIM].astype(BF16)


def backward_body(
    kv_heads, meta, query_ref, raw_ref, grad_ref, out_ref, inverse_ref, kv_ref,
    terms_ref, queries_ref, running_ref, delta_ref,
):
    heads, rows, _ = query_ref.shape
    group = heads // kv_heads
    running_ref[...] = jnp.zeros_like(running_ref)
    terms_ref[...] = jnp.zeros_like(terms_ref)
    for head in range(heads):
        product = grad_ref[head].astype(F32) * out_ref[
            :, head * HEAD_DIM : (head + 1) * HEAD_DIM
        ].astype(F32)
        delta_ref[head] = jnp.broadcast_to(jnp.sum(product, axis=1, keepdims=True), (rows, HEAD_DIM))

    def step(block, carry):
        allowed = allowed_block(meta, block, rows)
        span = pl.ds(pl.multiple_of(block * rows, rows), rows)
        for kv_head in range(kv_heads):
            key = kv_ref[span, kv_head * HEAD_DIM : (kv_head + 1) * HEAD_DIM]
            first = (kv_heads + kv_head) * HEAD_DIM
            value = kv_ref[span, first : first + HEAD_DIM]
            grad_key = jnp.zeros((rows, HEAD_DIM), F32)
            grad_value = jnp.zeros((rows, HEAD_DIM), F32)
            for head in range(kv_head * group, (kv_head + 1) * group):
                score = dot(query_ref[head], key, NT)
                probs = jnp.where(
                    allowed, jnp.exp(score_scale * score) * inverse_ref[head][:, :1], 0.0
                )
                grad_probs = dot(grad_ref[head], value, NT)
                grad_scores = (probs * (grad_probs - delta_ref[head][:, :1])).astype(BF16)
                running_ref[head] += dot(grad_scores, key, NN)
                grad_key = grad_key + dot(grad_scores, query_ref[head], TN)
                grad_value = grad_value + dot(probs.astype(BF16), grad_ref[head], TN)
            terms_ref[span, kv_head * HEAD_DIM : (kv_head + 1) * HEAD_DIM] = (
                score_scale * grad_key
            ).astype(BF16)
            terms_ref[span, first : first + HEAD_DIM] = grad_value.astype(BF16)
        return carry

    lax.fori_loop(meta[2], meta[0] + 1, step, 0)
    for head in range(heads):
        queries_ref[:, head * HEAD_DIM : (head + 1) * HEAD_DIM] = unit_back(
            raw_ref[head], score_scale * running_ref[head]
        ).astype(BF16)


def key_grad_body(raw_ref, grad_ref, out_ref):
    half = raw_ref.shape[1]
    for first in range(0, half, HEAD_DIM):
        cols = slice(first, first + HEAD_DIM)
        out_ref[:, cols] = unit_back(raw_ref[:, cols], grad_ref[:, cols].astype(F32)).astype(BF16)
    out_ref[:, half:] = grad_ref[:, half:]


def split_body(count, transposed, dotted, me_ref, left_ref, weight_ref, *refs):
    pieces = refs[:count] if dotted else ()
    refs = refs[len(pieces) :]
    outs = refs[:count]
    width = outs[0].shape[1]
    total = 0.0
    for step in list(range(1, count)) + [0]:
        span = pl.ds(offset(me_ref[0], count, step, width), width)
        if transposed:
            part = dot(left_ref[...], weight_ref[span, :], NT).astype(BF16)
        else:
            part = dot(left_ref[...], weight_ref[:, span], NN).astype(BF16)
        outs[step][...] = part
        if dotted:
            total = total + jnp.sum(
                part.astype(F32) * pieces[step][...].astype(F32), axis=1, keepdims=True
            )
    if dotted:
        refs[count][...] = jnp.broadcast_to(total, refs[count].shape)


def on_device(
    h_in,
    memory,
    cotangent,
    block_docs,
    w_query,
    w_out,
    self_key_value_weight,
    cache_key_value_weight,
):
    section_id = lax.axis_index("section")
    section_count = lax.axis_size("section")
    shard_id = lax.axis_index("seq")
    tp_id = lax.axis_index("tp")
    tp_count = lax.axis_size("tp")
    self_section = section_id == 0
    hidden = h_in[0]
    grad_local = cotangent[0]
    source = jnp.where(self_section, hidden, memory[0])

    def gathered(own):
        return [own] + [shifted(own, "tp", step) for step in range(1, tp_count)]

    source_pieces = gathered(source)
    hidden_pieces = gathered(hidden)
    grad_pieces = gathered(grad_local)

    rows, width = hidden.shape
    model = width * tp_count
    per = rows // BLK
    query_weight = w_query[0]
    out_weight = w_out[0]
    kv_weight = jnp.where(self_section, self_key_value_weight, cache_key_value_weight)
    kv_cols = self_key_value_weight.shape[2]
    kv_heads = kv_cols // HEAD_DIM
    query_cols = query_weight.shape[1]
    heads = query_cols // HEAD_DIM
    kv_flat = kv_weight.reshape(model, 2 * kv_cols)
    me = tp_id.astype(jnp.int32).reshape(1)

    all_docs = lax.all_gather(block_docs[0], "seq", axis=0, tiled=True)
    first_doc = lax.dynamic_slice_in_dim(all_docs, shard_id * per, 1)[0]
    first_block = jnp.sum((all_docs < first_doc).astype(jnp.int32)) // per
    window_block = jnp.maximum(shard_id * rows - WIN + 1, 0) // rows
    first_block = jnp.where(self_section, jnp.maximum(first_block, window_block), first_block)
    meta = jnp.concatenate(
        [
            jnp.stack([shard_id, self_section.astype(jnp.int32), first_block]).astype(jnp.int32),
            all_docs,
        ]
    )

    source_normed, source_factor, packed, key_raw = call(
        functools.partial(key_body, tp_count),
        [
            struct((rows, model), BF16),
            struct((rows, HEAD_DIM), F32),
            struct((rows, 2 * kv_cols), BF16),
            struct((rows, kv_cols), F32),
        ],
        [me, *source_pieces, kv_flat],
        1,
        2 * rows * model * 2 * kv_cols,
    )
    all_kv = lax.all_gather(packed, "seq", axis=0, tiled=True)
    length = all_kv.shape[0]

    normed, row_factor, query_unit, query_raw = call(
        functools.partial(query_body, tp_count),
        [
            struct((rows, model), BF16),
            struct((rows, HEAD_DIM), F32),
            struct((heads, rows, HEAD_DIM), BF16),
            struct((heads, rows, HEAD_DIM), F32),
        ],
        [me, *hidden_pieces, query_weight],
        1,
        2 * rows * model * query_cols,
    )
    attn_flat, inverse = call(
        functools.partial(forward_body, kv_heads),
        [struct((rows, query_cols), BF16), struct((heads, rows, HEAD_DIM), F32)],
        [meta, query_unit, all_kv],
        1,
        4 * rows * length * query_cols,
        [pltpu.VMEM((heads, rows, HEAD_DIM), F32)] * 2,
    )
    grad_rows, grad_attn = call(
        functools.partial(grad_attn_body, tp_count),
        [struct((rows, model), BF16), struct((heads, rows, HEAD_DIM), BF16)],
        [me, *grad_pieces, out_weight],
        1,
        2 * rows * model * query_cols,
    )
    kv_terms, grad_queries = call(
        functools.partial(backward_body, kv_heads),
        [struct((length, 2 * kv_cols), BF16), struct((rows, query_cols), BF16)],
        [meta, query_unit, query_raw, grad_attn, attn_flat, inverse, all_kv],
        1,
        10 * rows * length * query_cols,
        [pltpu.VMEM((heads, rows, HEAD_DIM), F32)] * 2,
    )

    def summed(parts):
        total = parts[0].astype(F32)
        for step in range(1, tp_count):
            total = total + shifted(parts[step], "tp", -step).astype(F32)
        return total

    def summed_dot(value):
        own = value[:, 0]
        total = own
        for step in range(1, tp_count):
            total = total + shifted(own, "tp", step)
        return total

    pieces_out = [struct((rows, width), BF16)] * tp_count
    projected = summed(
        call(
            functools.partial(split_body, tp_count, False, False),
            pieces_out,
            [me, attn_flat, out_weight],
            1,
            2 * rows * model * query_cols,
        )
    )
    h_out = (hidden.astype(F32) + projected).astype(BF16)
    passed = shifted(h_out, "section", 1)

    kv_grads = lax.psum_scatter(kv_terms, "seq", scatter_dimension=0, tiled=True)

    *rows_parts, row_dot = call(
        functools.partial(split_body, tp_count, True, True),
        pieces_out + [struct((rows, HEAD_DIM), F32)],
        [me, grad_queries, query_weight, *hidden_pieces],
        1,
        2 * rows * model * query_cols,
    )
    rows_part = summed(rows_parts)
    row_total = summed_dot(row_dot)
    hidden_wide = hidden.astype(F32)
    factor = row_factor[:, 0]
    grad_input = (
        grad_local.astype(F32)
        + factor[:, None] * rows_part
        - hidden_wide * (factor * factor * factor * row_total / model)[:, None]
    )

    (kv_grad,) = call(
        key_grad_body, [struct((rows, 2 * kv_cols), BF16)], [key_raw, kv_grads], 0, rows * kv_cols
    )
    *source_parts, source_dot = call(
        functools.partial(split_body, tp_count, True, True),
        pieces_out + [struct((rows, HEAD_DIM), F32)],
        [me, kv_grad, kv_flat, *source_pieces],
        1,
        4 * rows * model * kv_cols,
    )
    source_part = summed(source_parts)
    source_total = summed_dot(source_dot)
    source_wide = source.astype(F32)
    src = source_factor[:, 0]
    grad_memory = (
        src[:, None] * source_part
        - source_wide * (src * src * src * source_total / model)[:, None]
    )

    def over_tokens(left, right):
        return lax.psum_scatter(
            dot(left, right, TN).astype(BF16), "seq", scatter_dimension=0, tiled=True
        )

    out_share = over_tokens(grad_rows, attn_flat).astype(F32)
    query_share = over_tokens(normed, grad_queries).astype(F32)
    kv_share = over_tokens(source_normed, kv_grad)

    share_rows = kv_share.shape[0] // section_count
    own = lax.dynamic_slice_in_dim(kv_share, section_id * share_rows, share_rows, 0)
    self_grad = jnp.where(self_section, own, 0.0).astype(F32)
    cache_grad = jnp.where(self_section, 0.0, own).astype(F32)
    for step in range(1, section_count):
        target = lax.rem(section_id + step, section_count)
        piece = lax.dynamic_slice_in_dim(kv_share, target * share_rows, share_rows, 0)
        came = shifted(piece, "section", step).astype(F32)
        from_self = section_id == step
        self_grad = self_grad + jnp.where(from_self, came, 0.0)
        cache_grad = cache_grad + jnp.where(from_self, 0.0, came)
    return (
        passed[None],
        grad_input.astype(BF16)[None],
        grad_memory.astype(BF16)[None],
        query_share[None],
        out_share.T[None],
        self_grad.reshape(share_rows, 2, kv_cols),
        cache_grad.reshape(share_rows, 2, kv_cols),
    )


def solution(mesh):
    return jax.shard_map(
        on_device,
        mesh=mesh,
        in_specs=(
            P("section", "seq", "tp"),
            P("section", "seq", "tp"),
            P("section", "seq", "tp"),
            P("section", "seq"),
            P("section", None, "tp"),
            P("section", "tp", None),
            P(None, None, "tp"),
            P(None, None, "tp"),
        ),
        out_specs=(
            P("section", "seq", "tp"),
            P("section", "seq", "tp"),
            P("section", "seq", "tp"),
            P("section", "seq", "tp"),
            P("section", "tp", "seq"),
            P(("seq", "section"), None, "tp"),
            P(("seq", "section"), None, "tp"),
        ),
        check_vma=False,
    )
```

```python
import functools
import math

import jax
import jax.numpy as jnp
from jax import lax
from jax.experimental import pallas as pl
from jax.experimental.pallas import tpu as pltpu
from jax.sharding import PartitionSpec as P

HEAD_DIM = 128
BLK = 128
WIN = 1024

score_scale = 40.0
norm_eps = 1e-06
log2_e = math.log2(math.e)

F32 = jnp.float32
BF16 = jnp.bfloat16
NN = (((1,), (0,)), ((), ()))
NT = (((1,), (1,)), ((), ()))
TN = (((0,), (0,)), ((), ()))

VMEM = pl.BlockSpec(memory_space=pltpu.VMEM)
SMEM = pl.BlockSpec(memory_space=pltpu.SMEM)


def dot(left, right, dims):
    return lax.dot_general(left, right, dims, preferred_element_type=F32)


def shifted(value, axis, steps):
    count = lax.axis_size(axis)
    pairs = [(source, (source + steps) % count) for source in range(count)]
    return lax.ppermute(value, axis, pairs)


def call(
    body, out_shape, inputs, smem_count, flops, scratch=(), limit=60, after=(),
    grid=(), in_specs=None, out_specs=None,
):
    moved = sum(v.size * v.dtype.itemsize for v in inputs) + sum(
        o.size * o.dtype.itemsize for o in out_shape
    )
    if in_specs is None:
        in_specs = [SMEM] * smem_count + [VMEM] * (len(inputs) - smem_count)
    if out_specs is None:
        out_specs = [VMEM] * len(out_shape)

    def with_order(*refs):
        body(*refs[: len(inputs)], *refs[len(inputs) + len(after) :])

    return pl.pallas_call(
        with_order,
        out_shape=out_shape,
        grid=grid,
        in_specs=list(in_specs) + [pl.BlockSpec(memory_space=pl.ANY)] * len(after),
        out_specs=out_specs,
        scratch_shapes=list(scratch),
        compiler_params=pltpu.CompilerParams(vmem_limit_bytes=limit * 1024 * 1024),
        cost_estimate=pl.CostEstimate(flops=flops, bytes_accessed=moved, transcendentals=0),
    )(*inputs, *after)


def struct(shape, dtype):
    return jax.ShapeDtypeStruct(shape, dtype)


def offset(me, count, step, width):
    return pl.multiple_of(lax.rem(me + count - step, count) * width, width)


def normalize(pieces, me, normed_ref, factor_ref):
    count = len(pieces)
    width = pieces[0].shape[1]
    total = 0.0
    for piece in pieces:
        wide = piece[...].astype(F32)
        total = total + jnp.sum(wide * wide, axis=1, keepdims=True)
    factor = lax.rsqrt(total / (count * width) + norm_eps)
    factor_ref[...] = jnp.broadcast_to(factor, factor_ref.shape)
    for step, piece in enumerate(pieces):
        normed_ref[:, pl.ds(offset(me, count, step, width), width)] = (
            piece[...].astype(F32) * factor
        ).astype(BF16)


def unit(raw):
    return raw * lax.rsqrt(jnp.sum(raw * raw, axis=1, keepdims=True) + norm_eps)


def unit_back(raw, grad):
    scale = lax.rsqrt(jnp.sum(raw * raw, axis=1, keepdims=True) + norm_eps)
    along = jnp.sum(raw * grad, axis=1, keepdims=True)
    return scale * grad - raw * (scale * scale * scale * along)


def query_body(count, me_ref, *refs):
    pieces, (weight, normed_ref, factor_ref, unit_ref, raw_ref) = refs[:count], refs[count:]

    @pl.when(pl.program_id(0) == 0)
    def first():
        normalize(pieces, me_ref[0], normed_ref, factor_ref)

    both = dot(normed_ref[...], weight[...], NN)
    for head in range(unit_ref.shape[0]):
        raw = both[:, head * HEAD_DIM : (head + 1) * HEAD_DIM]
        raw_ref[head] = raw
        unit_ref[head] = unit(raw).astype(BF16)


def key_body(count, me_ref, *refs):
    pieces, (weight, normed_ref, factor_ref, packed_ref, raw_ref) = refs[:count], refs[count:]
    normalize(pieces, me_ref[0], normed_ref, factor_ref)
    both = dot(normed_ref[...], weight[...], NN)
    half = both.shape[1] // 2
    for head in range(half // HEAD_DIM):
        cols = slice(head * HEAD_DIM, (head + 1) * HEAD_DIM)
        packed_ref[:, cols] = unit(both[:, cols]).astype(BF16)
    packed_ref[:, half:] = both[:, half:].astype(BF16)
    raw_ref[...] = both[:, :half]


def allowed_block(meta, block, rows):
    per = rows // BLK
    shard, self_section = meta[0], meta[1]
    shape = (rows, rows)
    query = lax.broadcasted_iota(jnp.int32, shape, 0)
    key = lax.broadcasted_iota(jnp.int32, shape, 1)
    query_doc = jnp.full(shape, meta[3 + shard * per], jnp.int32)
    key_doc = jnp.full(shape, meta[3 + block * per], jnp.int32)
    for part in range(1, per):
        query_doc = jnp.where(query >= part * BLK, meta[3 + shard * per + part], query_doc)
        key_doc = jnp.where(key >= part * BLK, meta[3 + block * per + part], key_doc)
    query_pos = shard * rows + query
    key_pos = block * rows + key
    is_self = jnp.full(shape, self_section, jnp.int32) == 1
    upper = jnp.where(is_self, query_pos, query_pos // BLK * BLK + BLK - 1)
    lower = jnp.where(is_self, query_pos - WIN, -1)
    return (query_doc == key_doc) & (key_pos <= upper) & (key_pos > lower)


def key_value(kv_ref, span, kv_head, kv_heads):
    first = (kv_heads + kv_head) * HEAD_DIM
    key = kv_ref[span, kv_head * HEAD_DIM : (kv_head + 1) * HEAD_DIM]
    return key, kv_ref[span, first : first + HEAD_DIM]


def forward_body(kv_heads, meta, query_ref, kv_ref, out_ref, log_ref, number_ref, denom_ref):
    heads, rows, _ = query_ref.shape
    group = heads // kv_heads
    stacked = (group * rows, HEAD_DIM)
    number_ref[...] = jnp.zeros_like(number_ref)
    denom_ref[...] = jnp.zeros_like(denom_ref)

    def step(block, carry):
        allowed = allowed_block(meta, block, rows)
        span = pl.ds(pl.multiple_of(block * rows, rows), rows)
        for kv_head in range(kv_heads):
            mine = slice(kv_head * group, (kv_head + 1) * group)
            key, value = key_value(kv_ref, span, kv_head, kv_heads)
            score = dot(query_ref[mine].reshape(stacked), key, NT).reshape(group, rows, rows)
            weight = jnp.where(allowed[None], jnp.exp2(score * (score_scale * log2_e)), 0.0)
            folded = weight[:, :, :HEAD_DIM]
            for first in range(HEAD_DIM, rows, HEAD_DIM):
                folded = folded + weight[:, :, first : first + HEAD_DIM]
            denom_ref[mine] += folded
            product = dot(weight.astype(BF16).reshape(group * rows, rows), value, NN)
            number_ref[mine] += product.reshape(group, rows, HEAD_DIM)
        return carry

    lax.fori_loop(meta[2], meta[0] + 1, step, 0)
    for head in range(heads):
        denom = jnp.sum(denom_ref[head], axis=1, keepdims=True)
        log_ref[head] = jnp.broadcast_to(jnp.log2(denom), (rows, HEAD_DIM))
        out_ref[:, head * HEAD_DIM : (head + 1) * HEAD_DIM] = (number_ref[head] / denom).astype(BF16)


def rows_body(count, me_ref, *refs):
    width = refs[0].shape[1]
    for step, piece in enumerate(refs[:count]):
        refs[-1][:, pl.ds(offset(me_ref[0], count, step, width), width)] = piece[...]


def whole_rows(pieces, me, after):
    rows, width = pieces[0].shape
    (out,) = call(
        functools.partial(rows_body, len(pieces)),
        [struct((rows, width * len(pieces)), BF16)],
        [me, *pieces],
        1,
        0,
        after=after,
    )
    return out


def grad_attn_body(rows_ref, weight, grad_ref):
    both = dot(rows_ref[...], weight[...], NT)
    for head in range(grad_ref.shape[0]):
        grad_ref[head] = both[:, head * HEAD_DIM : (head + 1) * HEAD_DIM].astype(BF16)


def backward_body(
    kv_heads, meta, query_ref, raw_ref, grad_ref, out_ref, log_ref, kv_ref,
    keep_ref, *refs,
):
    *send_refs, queries_ref, running_ref, delta_ref = refs
    heads, rows, _ = query_ref.shape
    group = heads // kv_heads
    stacked = (group * rows, HEAD_DIM)
    running_ref[...] = jnp.zeros_like(running_ref)
    keep_ref[...] = jnp.zeros_like(keep_ref)
    for send_ref in send_refs:
        send_ref[...] = jnp.zeros_like(send_ref)
    for head in range(heads):
        cols = slice(head * HEAD_DIM, (head + 1) * HEAD_DIM)
        product = grad_ref[head].astype(F32) * out_ref[:, cols].astype(F32)
        delta_ref[head] = jnp.broadcast_to(jnp.sum(product, axis=1, keepdims=True), (rows, HEAD_DIM))

    def widened(ref, mine):
        return jnp.concatenate([ref[mine].reshape(stacked)] * (rows // HEAD_DIM), axis=1)

    def step(block, carry):
        allowed = allowed_block(meta, block, rows)
        span = pl.ds(pl.multiple_of(block * rows, rows), rows)
        for kv_head in range(kv_heads):
            mine = slice(kv_head * group, (kv_head + 1) * group)
            key, value = key_value(kv_ref, span, kv_head, kv_heads)
            query = query_ref[mine].reshape(stacked)
            grad = grad_ref[mine].reshape(stacked)
            score = dot(query, key, NT)
            probs = jnp.exp2(score * (score_scale * log2_e) - widened(log_ref, mine))
            probs = jnp.where(allowed[None], probs.reshape(group, rows, rows), 0.0)
            probs = probs.reshape(group * rows, rows)
            grad_probs = dot(grad, value, NT)
            grad_scores = (probs * (grad_probs - widened(delta_ref, mine))).astype(BF16)
            running_ref[mine] += dot(grad_scores, key, NN).reshape(group, rows, HEAD_DIM)
            key_term = (score_scale * dot(grad_scores, query, TN)).astype(BF16)
            value_term = dot(probs.astype(BF16), grad, TN).astype(BF16)
            low = kv_head * HEAD_DIM
            high = (kv_heads + kv_head) * HEAD_DIM

            steps = meta[0] // 2 - block // 2
            same_core = block % 2 == meta[0] % 2

            @pl.when(same_core)
            def own():
                keep_ref[steps, :, low : low + HEAD_DIM] = key_term
                keep_ref[steps, :, high : high + HEAD_DIM] = value_term

            for place, send_ref in enumerate(send_refs):

                def other(send_ref=send_ref):
                    send_ref[:, low : low + HEAD_DIM] = key_term
                    send_ref[:, high : high + HEAD_DIM] = value_term

                pl.when(jnp.logical_not(same_core) & (steps == place))(other)
        return carry

    lax.fori_loop(meta[2], meta[0] + 1, step, 0)
    for head in range(heads):
        queries_ref[:, head * HEAD_DIM : (head + 1) * HEAD_DIM] = unit_back(
            raw_ref[head], score_scale * running_ref[head]
        ).astype(BF16)


CHUNKS = 1


def chunked(rows):
    return CHUNKS if rows % (16 * CHUNKS) == 0 else 1


def split(count, transposed, me, left, weight_ref, pieces, outs, dot_ref):
    own_ref, sent = outs[0], outs[1:]
    rows, width = own_ref.shape
    parts = len(sent) // max(count - 1, 1)
    total = 0.0
    for step in list(range(1, count)) + [0]:
        span = pl.ds(offset(me, count, step, width), width)
        if transposed:
            part = dot(left, weight_ref[span, :], NT).astype(BF16)
        else:
            part = dot(left, weight_ref[:, span], NN).astype(BF16)
        if step == 0:
            own_ref[...] = part
        else:
            tall = rows // parts
            for index in range(parts):
                sent[(step - 1) * parts + index][...] = part[index * tall : (index + 1) * tall]
        if dot_ref is not None:
            total = total + jnp.sum(
                part.astype(F32) * pieces[step][...].astype(F32), axis=1, keepdims=True
            )
    if dot_ref is not None:
        dot_ref[...] = jnp.broadcast_to(total, dot_ref.shape)


def split_shapes(rows, width, count):
    parts = chunked(rows)
    return [struct((rows, width), BF16)] + [struct((rows // parts, width), BF16)] * (
        parts * (count - 1)
    )


def sent_over_tp(outs, rows):
    parts = chunked(rows)
    return [shifted(out, "tp", -(1 + index // parts)) for index, out in enumerate(outs[1:])]


def project_body(count, me_ref, left_ref, weight_ref, *outs):
    split(count, False, me_ref[0], left_ref[...], weight_ref, None, outs, None)


def back_body(count, me_ref, left_ref, weight_ref, *refs):
    pieces, outs, dot_ref = refs[:count], refs[count:-1], refs[-1]
    split(count, True, me_ref[0], left_ref[...], weight_ref, pieces, outs, dot_ref)


def key_back_body(count, terms, me_ref, raw_ref, weight_ref, *refs):
    term_refs, refs = refs[:terms], refs[terms:]
    pieces, outs, dot_ref, grad_ref = refs[:count], refs[count:-2], refs[-2], refs[-1]
    half = raw_ref.shape[1]
    total = term_refs[0][...].astype(F32)
    for term in term_refs[1:]:
        total = total + term[...].astype(F32)
    for first in range(0, half, HEAD_DIM):
        cols = slice(first, first + HEAD_DIM)
        grad_ref[:, cols] = unit_back(raw_ref[:, cols], total[:, cols]).astype(BF16)
    grad_ref[:, half:] = total[:, half:].astype(BF16)
    split(count, True, me_ref[0], grad_ref[...], weight_ref, pieces, outs, dot_ref)


def summed(own_ref, came, at):
    rows = own_ref.shape[0]
    parts = chunked(rows)
    tall = rows // parts
    total = own_ref[at * tall : (at + 1) * tall].astype(F32)
    for ref in came[at::parts]:
        total = total + ref[...].astype(F32)
    return total, slice(at * tall, (at + 1) * tall)


def output_body(hidden_ref, own_ref, *refs):
    came, out_ref = refs[:-1], refs[-1]
    for at in range(chunked(own_ref.shape[0])):
        total, span = summed(own_ref, came, at)
        out_ref[span] = (hidden_ref[span].astype(F32) + total).astype(BF16)


def input_body(count, residual, model, *refs):
    base, refs = (refs[0], refs[1:]) if residual else (None, refs)
    values_ref, factor_ref, own_ref, *refs = refs
    dots, came, out_ref = refs[:count], refs[count:-1], refs[-1]
    for at in range(chunked(own_ref.shape[0])):
        total, span = summed(own_ref, came, at)
        dot_total = dots[0][span, :1]
        for ref in dots[1:]:
            dot_total = dot_total + ref[span, :1]
        factor = factor_ref[span, :1]
        grad = factor * total - values_ref[span].astype(F32) * (
            factor * factor * factor * dot_total / model
        )
        if residual:
            grad = grad + base[span].astype(F32)
        out_ref[span] = grad.astype(BF16)


def flipped_bits(value, count):
    out, left = 0, count
    while left > 1:
        out = out * 2 + value % 2
        value, left = value // 2, left // 2
    return out


def tokens_body(at_ref, left_ref, right_ref, keep_ref, *send_refs):
    both = dot(left_ref[...], right_ref[...], TN).astype(BF16)
    half = both.shape[0] // 2

    @pl.when(at_ref[0] == 0)
    def low():
        keep_ref[0] = both[:half]

    @pl.when(at_ref[0] == 1)
    def high():
        keep_ref[0] = both[half:]

    for place, send_ref in enumerate(send_refs):

        @pl.when((at_ref[0] == 0) & (pl.program_id(0) == place))
        def low_sent(send_ref=send_ref):
            send_ref[...] = both[half:]

        @pl.when((at_ref[0] == 1) & (pl.program_id(0) == place))
        def high_sent(send_ref=send_ref):
            send_ref[...] = both[:half]


def ordered(body, inputs, after, outs, grid, in_specs, out_specs, scalars):
    kept = 1 + len(inputs)

    def with_order(*refs):
        body(*refs[:kept], *refs[kept + len(after) :])

    return pl.pallas_call(
        with_order,
        out_shape=outs,
        grid_spec=pltpu.PrefetchScalarGridSpec(
            num_scalar_prefetch=1,
            grid=grid,
            in_specs=in_specs + [pl.BlockSpec(memory_space=pl.ANY)] * len(after),
            out_specs=out_specs,
        ),
        compiler_params=pltpu.CompilerParams(vmem_limit_bytes=60 * 1024 * 1024),
        cost_estimate=pl.CostEstimate(flops=0, bytes_accessed=1024, transcendentals=0),
    )(scalars, *inputs, *after)


def over_tokens(left, right, after=()):
    rows, model = left.shape
    chips = lax.axis_size("seq") // 2
    step = model // chips
    cols = right.shape[1]
    shard = lax.axis_index("seq").astype(jnp.int32)
    near = jnp.stack(
        [shard % 2]
        + [lax.bitwise_xor(shard // 2, jnp.int32(flipped_bits(i, chips))) for i in range(chips)]
    )
    share = (step // 2, cols)
    keep, *send = ordered(
        tokens_body,
        [left, right],
        after,
        [struct((chips, *share), BF16)] + [struct(share, BF16)] * chips,
        (chips,),
        [
            pl.BlockSpec((rows, step), lambda i, at: (0, at[1 + i])),
            pl.BlockSpec(right.shape, lambda i, at: (0, 0)),
        ],
        [pl.BlockSpec((1, *share), lambda i, at: (i, 0, 0))]
        + [pl.BlockSpec(share, lambda i, at: (0, 0))] * chips,
        near,
    )
    return keep, send


def add_body(count, at_ref, *refs):
    out_ref = refs[-1]
    for index in range(count):
        total = refs[0][index].astype(F32) + refs[1 + index][...].astype(F32)
        for ref in refs[1 + count : -1]:
            total = total + ref[index].astype(F32)
        out_ref[index] = total.astype(out_ref.dtype)


def added(keep, came, terms, first, count, dtype, after):
    rows, cols = keep.shape[1:]
    block = pl.BlockSpec((count, rows, cols), lambda i, at: (first // count, 0, 0))
    flat = pl.BlockSpec((rows, cols), lambda i, at: (0, 0))
    (out,) = ordered(
        functools.partial(add_body, count),
        [keep, *came[first : first + count], *terms],
        after,
        [struct((count, rows, cols), dtype)],
        (1,),
        [block] + [flat] * count + [block] * len(terms),
        [pl.BlockSpec((count, rows, cols), lambda i, at: (0, 0, 0))],
        jnp.zeros((1,), jnp.int32),
    )
    return out


def whole_body(left_ref, right_ref, out_ref):
    out_ref[...] = dot(left_ref[...], right_ref[...], TN).astype(BF16)


def scattered(left, right, after=()):
    rows, model = left.shape
    step = math.gcd(model, 512)
    cols = right.shape[1]
    (partial,) = call(
        whole_body,
        [struct((model, cols), BF16)],
        [left, right],
        0,
        2 * rows * model * cols,
        after=after,
        grid=(model // step,),
        in_specs=[
            pl.BlockSpec((rows, step), lambda i: (0, i)),
            pl.BlockSpec(right.shape, lambda i: (0, 0)),
        ],
        out_specs=[pl.BlockSpec((step, cols), lambda i: (i, 0))],
    )
    return lax.psum_scatter(partial, "seq", scatter_dimension=0, tiled=True), partial


def core_swap(value):
    count = lax.axis_size("seq")
    return lax.ppermute(value, "seq", [(shard, shard ^ 1) for shard in range(count)])


def chip_sum_body(count, keep_ref, *refs):
    for index in range(count):
        total = keep_ref[index].astype(F32) + refs[index][...].astype(F32)
        refs[count + index][...] = total.astype(BF16)


def sums_below(keep, came, after):
    chips, rows, cols = keep.shape
    sums = call(
        functools.partial(chip_sum_body, chips),
        [struct((rows, cols), BF16)] * chips,
        [keep, *came],
        0,
        2 * keep.size,
        after=after,
    )
    terms = [sums[0]]
    for steps in range(1, chips):
        pairs = [(shard, shard - 2 * steps) for shard in range(2 * steps, 2 * chips)]
        terms.append(lax.ppermute(sums[steps], "seq", pairs))
    return terms, sums[0]


class Halving:
    def __init__(self, keep, send):
        self.keep = keep
        self.came = [core_swap(piece) for piece in send]
        self.terms = []
        self.count = keep.shape[0]
        self.distance = 2

    def step(self, after):
        self.count //= 2
        sent = added(self.keep, self.came, self.terms, self.count, self.count, BF16, after)
        pairs = [(shard, shard ^ self.distance) for shard in range(lax.axis_size("seq"))]
        self.terms.append(lax.ppermute(sent, "seq", pairs))
        self.distance *= 2
        return sent

    def last(self, after):
        return added(self.keep, self.came, self.terms, 0, 1, F32, after)[0]


def on_device(
    h_in,
    memory,
    cotangent,
    block_docs,
    w_query,
    w_out,
    self_key_value_weight,
    cache_key_value_weight,
):
    section_id = lax.axis_index("section")
    section_count = lax.axis_size("section")
    shard_id = lax.axis_index("seq")
    tp_id = lax.axis_index("tp")
    tp_count = lax.axis_size("tp")
    self_section = section_id == 0
    hidden = h_in[0]
    grad_local = cotangent[0]
    source = jnp.where(self_section, hidden, memory[0])

    def gathered(own):
        return [own] + [shifted(own, "tp", step) for step in range(1, tp_count)]

    source_pieces = gathered(source)
    hidden_pieces = gathered(hidden)
    grad_pieces = gathered(grad_local)

    rows, width = hidden.shape
    model = width * tp_count
    per = rows // BLK
    query_weight = w_query[0]
    out_weight = w_out[0]
    kv_weight = jnp.where(self_section, self_key_value_weight, cache_key_value_weight)
    kv_cols = self_key_value_weight.shape[2]
    kv_heads = kv_cols // HEAD_DIM
    query_cols = query_weight.shape[1]
    heads = query_cols // HEAD_DIM
    kv_flat = kv_weight.reshape(model, 2 * kv_cols)
    me = tp_id.astype(jnp.int32).reshape(1)

    all_docs = lax.all_gather(block_docs[0], "seq", axis=0, tiled=True)
    first_doc = lax.dynamic_slice_in_dim(all_docs, shard_id * per, 1)[0]
    first_block = jnp.sum((all_docs < first_doc).astype(jnp.int32)) // per
    window_block = jnp.maximum(shard_id * rows - WIN + 1, 0) // rows
    first_block = jnp.where(self_section, jnp.maximum(first_block, window_block), first_block)
    meta = jnp.concatenate(
        [
            jnp.stack([shard_id, self_section.astype(jnp.int32), first_block]).astype(jnp.int32),
            all_docs,
        ]
    )

    source_normed, source_factor, packed, key_raw = call(
        functools.partial(key_body, tp_count),
        [
            struct((rows, model), BF16),
            struct((rows, HEAD_DIM), F32),
            struct((rows, 2 * kv_cols), BF16),
            struct((rows, kv_cols), F32),
        ],
        [me, *source_pieces, kv_flat],
        1,
        2 * rows * model * 2 * kv_cols,
        after=[meta],
    )
    all_kv = lax.all_gather(packed, "seq", axis=0, tiled=True)
    length = all_kv.shape[0]
    chips = length // rows // 2

    together = 2 if heads % 2 == 0 else 1
    whole = pl.BlockSpec((rows, width), lambda i: (0, 0))
    full = pl.BlockSpec((rows, model), lambda i: (0, 0))
    per_head = pl.BlockSpec((together, rows, HEAD_DIM), lambda i: (i, 0, 0))
    normed, row_factor, query_unit, query_raw = call(
        functools.partial(query_body, tp_count),
        [
            struct((rows, model), BF16),
            struct((rows, HEAD_DIM), F32),
            struct((heads, rows, HEAD_DIM), BF16),
            struct((heads, rows, HEAD_DIM), F32),
        ],
        [me, *hidden_pieces, query_weight],
        1,
        2 * rows * model * query_cols,
        after=[packed],
        grid=(heads // together,),
        in_specs=[SMEM]
        + [whole] * tp_count
        + [pl.BlockSpec((model, together * HEAD_DIM), lambda i: (0, i))],
        out_specs=[
            full,
            pl.BlockSpec((rows, HEAD_DIM), lambda i: (0, 0)),
            per_head,
            per_head,
        ],
    )
    attn_flat, log_denom = call(
        functools.partial(forward_body, kv_heads),
        [struct((rows, query_cols), BF16), struct((heads, rows, HEAD_DIM), F32)],
        [meta, query_unit, all_kv],
        1,
        4 * rows * length * query_cols,
        [pltpu.VMEM((heads, rows, HEAD_DIM), F32)] * 2,
    )
    grad_rows = whole_rows(grad_pieces, me, [attn_flat])
    out_share, mark = scattered(grad_rows, attn_flat)
    (grad_attn,) = call(
        grad_attn_body,
        [struct((heads, rows, HEAD_DIM), BF16)],
        [grad_rows, out_weight],
        0,
        2 * rows * model * query_cols,
        after=[mark],
        grid=(heads // together,),
        in_specs=[full]
        + [pl.BlockSpec((together * HEAD_DIM, model), lambda i: (i, 0))],
        out_specs=[per_head],
    )
    halves = [struct((chips, rows, 2 * kv_cols), BF16)] + [
        struct((rows, 2 * kv_cols), BF16)
    ] * chips
    keep, *send, grad_queries = call(
        functools.partial(backward_body, kv_heads),
        halves + [struct((rows, query_cols), BF16)],
        [meta, query_unit, query_raw, grad_attn, attn_flat, log_denom, all_kv],
        1,
        10 * rows * length * query_cols,
        [pltpu.VMEM((heads, rows, HEAD_DIM), F32)] * 2,
        after=[mark],
    )
    kv_came = [core_swap(piece) for piece in send]
    query_share, mark = scattered(normed, grad_queries)
    kv_sums, mark = sums_below(keep, kv_came, [mark])

    def dots(value):
        return [value] + [shifted(value, "tp", step) for step in range(1, tp_count)]

    wide = struct((rows, width), BF16)
    broad = struct((rows, HEAD_DIM), F32)
    shapes = split_shapes(rows, width, tp_count)
    projected = call(
        functools.partial(project_body, tp_count),
        shapes,
        [me, attn_flat, out_weight],
        1,
        2 * rows * model * query_cols,
        after=[mark],
    )
    projected_came = sent_over_tp(projected, rows)
    *rows_parts, row_dot = call(
        functools.partial(back_body, tp_count),
        shapes + [broad],
        [me, grad_queries, query_weight, *hidden_pieces],
        1,
        2 * rows * model * query_cols,
        after=[projected[0]],
    )
    rows_came = sent_over_tp(rows_parts, rows)
    row_dots = dots(row_dot)
    *source_parts, source_dot, kv_grad = call(
        functools.partial(key_back_body, tp_count, chips),
        shapes + [broad, struct((rows, 2 * kv_cols), BF16)],
        [me, key_raw, kv_flat, *kv_sums, *source_pieces],
        1,
        4 * rows * model * kv_cols,
        after=[row_dot],
    )
    source_came = sent_over_tp(source_parts, rows)
    source_dots = dots(source_dot)
    kv_keep, kv_send = over_tokens(source_normed, kv_grad)
    kv_sum = Halving(kv_keep, kv_send)
    (h_out,) = call(
        output_body, [wide], [hidden, projected[0], *projected_came], 0, 0, after=[kv_keep]
    )
    passed = shifted(h_out, "section", 1)
    mark = h_out
    while kv_sum.count > 2:
        mark = kv_sum.step([mark])
    (grad_input,) = call(
        functools.partial(input_body, tp_count, True, model),
        [wide],
        [grad_local, hidden, row_factor, rows_parts[0], *row_dots, *rows_came],
        0,
        0,
        after=[mark],
    )
    mark = kv_sum.step([grad_input])
    (grad_memory,) = call(
        functools.partial(input_body, tp_count, False, model),
        [wide],
        [source, source_factor, source_parts[0], *source_dots, *source_came],
        0,
        0,
        after=[mark],
    )
    kv_share = kv_sum.last([grad_memory])

    share_rows = kv_share.shape[0] // section_count
    own = lax.dynamic_slice_in_dim(kv_share, section_id * share_rows, share_rows, 0)
    self_grad = jnp.where(self_section, own, 0.0)
    cache_grad = jnp.where(self_section, 0.0, own)
    for step in range(1, section_count):
        target = lax.rem(section_id + step, section_count)
        piece = lax.dynamic_slice_in_dim(kv_share, target * share_rows, share_rows, 0)
        came = shifted(piece.astype(BF16), "section", step).astype(F32)
        from_self = section_id == step
        self_grad = self_grad + jnp.where(from_self, came, 0.0)
        cache_grad = cache_grad + jnp.where(from_self, 0.0, came)
    return (
        passed[None],
        grad_input[None],
        grad_memory[None],
        query_share.astype(F32)[None],
        out_share.astype(F32).T[None],
        self_grad.reshape(share_rows, 2, kv_cols),
        cache_grad.reshape(share_rows, 2, kv_cols),
    )


def solution(mesh):
    return jax.shard_map(
        on_device,
        mesh=mesh,
        in_specs=(
            P("section", "seq", "tp"),
            P("section", "seq", "tp"),
            P("section", "seq", "tp"),
            P("section", "seq"),
            P("section", None, "tp"),
            P("section", "tp", None),
            P(None, None, "tp"),
            P(None, None, "tp"),
        ),
        out_specs=(
            P("section", "seq", "tp"),
            P("section", "seq", "tp"),
            P("section", "seq", "tp"),
            P("section", "seq", "tp"),
            P("section", "tp", "seq"),
            P(("seq", "section"), None, "tp"),
            P(("seq", "section"), None, "tp"),
        ),
        check_vma=False,
    )
```

```python
import functools
import math

import jax
import jax.numpy as jnp
from jax import lax
from jax.experimental import pallas as pl
from jax.experimental.pallas import tpu as pltpu
from jax.sharding import PartitionSpec as P

HEAD_DIM = 128
BLK = 128
WIN = 1024

score_scale = 40.0
norm_eps = 1e-06
log2_e = math.log2(math.e)

F32 = jnp.float32
BF16 = jnp.bfloat16
NN = (((1,), (0,)), ((), ()))
NT = (((1,), (1,)), ((), ()))
TN = (((0,), (0,)), ((), ()))

VMEM = pl.BlockSpec(memory_space=pltpu.VMEM)
SMEM = pl.BlockSpec(memory_space=pltpu.SMEM)


def dot(left, right, dims):
    return lax.dot_general(left, right, dims, preferred_element_type=F32)


def shifted(value, axis, steps):
    count = lax.axis_size(axis)
    pairs = [(source, (source + steps) % count) for source in range(count)]
    return lax.ppermute(value, axis, pairs)


def call(
    body, out_shape, inputs, smem_count, flops, scratch=(), limit=60, after=(),
    grid=(), in_specs=None, out_specs=None,
):
    moved = sum(v.size * v.dtype.itemsize for v in inputs) + sum(
        o.size * o.dtype.itemsize for o in out_shape
    )
    if in_specs is None:
        in_specs = [SMEM] * smem_count + [VMEM] * (len(inputs) - smem_count)
    if out_specs is None:
        out_specs = [VMEM] * len(out_shape)

    def with_order(*refs):
        body(*refs[: len(inputs)], *refs[len(inputs) + len(after) :])

    return pl.pallas_call(
        with_order,
        out_shape=out_shape,
        grid=grid,
        in_specs=list(in_specs) + [pl.BlockSpec(memory_space=pl.ANY)] * len(after),
        out_specs=out_specs,
        scratch_shapes=list(scratch),
        compiler_params=pltpu.CompilerParams(vmem_limit_bytes=limit * 1024 * 1024),
        cost_estimate=pl.CostEstimate(flops=flops, bytes_accessed=moved, transcendentals=0),
    )(*inputs, *after)


def struct(shape, dtype):
    return jax.ShapeDtypeStruct(shape, dtype)


def offset(me, count, step, width):
    return pl.multiple_of(lax.rem(me + count - step, count) * width, width)


def normalize(pieces, me, normed_ref, factor_ref):
    count = len(pieces)
    width = pieces[0].shape[1]
    total = 0.0
    for piece in pieces:
        wide = piece[...].astype(F32)
        total = total + jnp.sum(wide * wide, axis=1, keepdims=True)
    factor = lax.rsqrt(total / (count * width) + norm_eps)
    factor_ref[...] = jnp.broadcast_to(factor, factor_ref.shape)
    for step, piece in enumerate(pieces):
        normed_ref[:, pl.ds(offset(me, count, step, width), width)] = (
            piece[...].astype(F32) * factor
        ).astype(BF16)


def unit(raw):
    return raw * lax.rsqrt(jnp.sum(raw * raw, axis=1, keepdims=True) + norm_eps)


def unit_back(raw, grad):
    scale = lax.rsqrt(jnp.sum(raw * raw, axis=1, keepdims=True) + norm_eps)
    along = jnp.sum(raw * grad, axis=1, keepdims=True)
    return scale * grad - raw * (scale * scale * scale * along)


def query_body(count, me_ref, *refs):
    pieces, (weight, normed_ref, factor_ref, unit_ref, raw_ref) = refs[:count], refs[count:]

    @pl.when(pl.program_id(0) == 0)
    def first():
        normalize(pieces, me_ref[0], normed_ref, factor_ref)

    both = dot(normed_ref[...], weight[...], NN)
    for head in range(unit_ref.shape[0]):
        raw = both[:, head * HEAD_DIM : (head + 1) * HEAD_DIM]
        raw_ref[head] = raw
        unit_ref[head] = unit(raw).astype(BF16)


def key_body(count, me_ref, *refs):
    pieces, (weight, normed_ref, factor_ref, packed_ref, raw_ref) = refs[:count], refs[count:]
    normalize(pieces, me_ref[0], normed_ref, factor_ref)
    both = dot(normed_ref[...], weight[...], NN)
    half = both.shape[1] // 2
    for head in range(half // HEAD_DIM):
        cols = slice(head * HEAD_DIM, (head + 1) * HEAD_DIM)
        packed_ref[:, cols] = unit(both[:, cols]).astype(BF16)
    packed_ref[:, half:] = both[:, half:].astype(BF16)
    raw_ref[...] = both[:, :half]


def allowed_block(meta, block, rows):
    per = rows // BLK
    shard, self_section = meta[0], meta[1]
    shape = (rows, rows)
    query = lax.broadcasted_iota(jnp.int32, shape, 0)
    key = lax.broadcasted_iota(jnp.int32, shape, 1)
    query_doc = jnp.full(shape, meta[3 + shard * per], jnp.int32)
    key_doc = jnp.full(shape, meta[3 + block * per], jnp.int32)
    for part in range(1, per):
        query_doc = jnp.where(query >= part * BLK, meta[3 + shard * per + part], query_doc)
        key_doc = jnp.where(key >= part * BLK, meta[3 + block * per + part], key_doc)
    query_pos = shard * rows + query
    key_pos = block * rows + key
    is_self = jnp.full(shape, self_section, jnp.int32) == 1
    upper = jnp.where(is_self, query_pos, query_pos // BLK * BLK + BLK - 1)
    lower = jnp.where(is_self, query_pos - WIN, -1)
    return (query_doc == key_doc) & (key_pos <= upper) & (key_pos > lower)


def key_value(kv_ref, span, kv_head, kv_heads):
    first = (kv_heads + kv_head) * HEAD_DIM
    key = kv_ref[span, kv_head * HEAD_DIM : (kv_head + 1) * HEAD_DIM]
    return key, kv_ref[span, first : first + HEAD_DIM]


def forward_body(kv_heads, meta, query_ref, kv_ref, out_ref, log_ref, number_ref, denom_ref):
    heads, rows, _ = query_ref.shape
    group = heads // kv_heads
    stacked = (group * rows, HEAD_DIM)
    number_ref[...] = jnp.zeros_like(number_ref)
    denom_ref[...] = jnp.zeros_like(denom_ref)

    def step(block, carry):
        allowed = allowed_block(meta, block, rows)
        span = pl.ds(pl.multiple_of(block * rows, rows), rows)
        for kv_head in range(kv_heads):
            mine = slice(kv_head * group, (kv_head + 1) * group)
            key, value = key_value(kv_ref, span, kv_head, kv_heads)
            score = dot(query_ref[mine].reshape(stacked), key, NT).reshape(group, rows, rows)
            weight = jnp.where(allowed[None], jnp.exp2(score * (score_scale * log2_e)), 0.0)
            folded = weight[:, :, :HEAD_DIM]
            for first in range(HEAD_DIM, rows, HEAD_DIM):
                folded = folded + weight[:, :, first : first + HEAD_DIM]
            denom_ref[mine] += folded
            product = dot(weight.astype(BF16).reshape(group * rows, rows), value, NN)
            number_ref[mine] += product.reshape(group, rows, HEAD_DIM)
        return carry

    lax.fori_loop(meta[2], meta[0] + 1, step, 0)
    for head in range(heads):
        denom = jnp.sum(denom_ref[head], axis=1, keepdims=True)
        log_ref[head] = jnp.broadcast_to(jnp.log2(denom), (rows, HEAD_DIM))
        out_ref[:, head * HEAD_DIM : (head + 1) * HEAD_DIM] = (number_ref[head] / denom).astype(BF16)


def grad_attn_body(count, me_ref, *refs):
    pieces, (weight, grad_ref) = refs[:count], refs[count:]
    width = pieces[0].shape[1]
    both = 0.0
    for step, piece in enumerate(pieces):
        span = pl.ds(offset(me_ref[0], count, step, width), width)
        both = both + dot(piece[...], weight[:, span], NT)
    for head in range(grad_ref.shape[0]):
        grad_ref[head] = both[:, head * HEAD_DIM : (head + 1) * HEAD_DIM].astype(BF16)


def backward_body(
    kv_heads, meta, query_ref, raw_ref, grad_ref, out_ref, log_ref, kv_ref,
    keep_ref, *refs,
):
    *send_refs, queries_ref, running_ref, delta_ref = refs
    heads, rows, _ = query_ref.shape
    group = heads // kv_heads
    stacked = (group * rows, HEAD_DIM)
    running_ref[...] = jnp.zeros_like(running_ref)
    keep_ref[...] = jnp.zeros_like(keep_ref)
    for send_ref in send_refs:
        send_ref[...] = jnp.zeros_like(send_ref)
    for head in range(heads):
        cols = slice(head * HEAD_DIM, (head + 1) * HEAD_DIM)
        product = grad_ref[head].astype(F32) * out_ref[:, cols].astype(F32)
        delta_ref[head] = jnp.broadcast_to(jnp.sum(product, axis=1, keepdims=True), (rows, HEAD_DIM))

    def widened(ref, mine):
        return jnp.concatenate([ref[mine].reshape(stacked)] * (rows // HEAD_DIM), axis=1)

    def step(block, carry):
        allowed = allowed_block(meta, block, rows)
        span = pl.ds(pl.multiple_of(block * rows, rows), rows)
        for kv_head in range(kv_heads):
            mine = slice(kv_head * group, (kv_head + 1) * group)
            key, value = key_value(kv_ref, span, kv_head, kv_heads)
            query = query_ref[mine].reshape(stacked)
            grad = grad_ref[mine].reshape(stacked)
            score = dot(query, key, NT)
            probs = jnp.exp2(score * (score_scale * log2_e) - widened(log_ref, mine))
            probs = jnp.where(allowed[None], probs.reshape(group, rows, rows), 0.0)
            probs = probs.reshape(group * rows, rows)
            grad_probs = dot(grad, value, NT)
            grad_scores = (probs * (grad_probs - widened(delta_ref, mine))).astype(BF16)
            running_ref[mine] += dot(grad_scores, key, NN).reshape(group, rows, HEAD_DIM)
            key_term = (score_scale * dot(grad_scores, query, TN)).astype(BF16)
            value_term = dot(probs.astype(BF16), grad, TN).astype(BF16)
            low = kv_head * HEAD_DIM
            high = (kv_heads + kv_head) * HEAD_DIM

            steps = meta[0] // 2 - block // 2
            same_core = block % 2 == meta[0] % 2

            @pl.when(same_core)
            def own():
                keep_ref[steps, :, low : low + HEAD_DIM] = key_term
                keep_ref[steps, :, high : high + HEAD_DIM] = value_term

            for place, send_ref in enumerate(send_refs):

                def other(send_ref=send_ref):
                    send_ref[:, low : low + HEAD_DIM] = key_term
                    send_ref[:, high : high + HEAD_DIM] = value_term

                pl.when(jnp.logical_not(same_core) & (steps == place))(other)
        return carry

    lax.fori_loop(meta[2], meta[0] + 1, step, 0)
    for head in range(heads):
        queries_ref[:, head * HEAD_DIM : (head + 1) * HEAD_DIM] = unit_back(
            raw_ref[head], score_scale * running_ref[head]
        ).astype(BF16)


def split(count, transposed, me, left, weight_ref, pieces, outs, dot_ref):
    rows, width = outs[0].shape
    total = 0.0
    for step in list(range(1, count)) + [0]:
        span = pl.ds(offset(me, count, step, width), width)
        if transposed:
            part = dot(left, weight_ref[span, :], NT).astype(BF16)
        else:
            part = dot(left, weight_ref[:, span], NN).astype(BF16)
        outs[step][:, :width] = part
        if dot_ref is not None:
            total = total + jnp.sum(
                part.astype(F32) * pieces[step][...].astype(F32), axis=1, keepdims=True
            )
    if dot_ref is not None:
        dot_ref[...] = jnp.broadcast_to(total, dot_ref.shape)
        lane = lax.broadcasted_iota(jnp.int32, dot_ref.shape, 1)
        rest, column = total, jnp.zeros(dot_ref.shape, F32)
        for place in range(3):
            term = rest.astype(BF16).astype(F32)
            column = jnp.where(lane == place, term, column)
            rest = rest - term
        for out in outs[1:]:
            out[:, width:] = column.astype(BF16)


def split_shapes(rows, width, count, dotted):
    extra = HEAD_DIM if dotted else 0
    return [struct((rows, width), BF16)] + [struct((rows, width + extra), BF16)] * (count - 1)


def sent_over_tp(outs):
    return [shifted(out, "tp", -1 - index) for index, out in enumerate(outs)]


def project_body(count, me_ref, left_ref, weight_ref, *outs):
    split(count, False, me_ref[0], left_ref[...], weight_ref, None, outs, None)


def back_body(count, me_ref, left_ref, weight_ref, *refs):
    pieces, outs, dot_ref = refs[:count], refs[count:-1], refs[-1]
    split(count, True, me_ref[0], left_ref[...], weight_ref, pieces, outs, dot_ref)


def key_grad_body(raw_ref, *refs):
    term_refs, grad_ref = refs[:-1], refs[-1]
    half = raw_ref.shape[1]
    total = sum(term[...].astype(F32) for term in term_refs)
    for first in range(0, half, HEAD_DIM):
        cols = slice(first, first + HEAD_DIM)
        grad_ref[:, cols] = unit_back(raw_ref[:, cols], total[:, cols]).astype(BF16)
    grad_ref[:, half:] = total[:, half:].astype(BF16)


def output_body(hidden_ref, own_ref, *refs):
    total = hidden_ref[...].astype(F32) + sum(ref[...].astype(F32) for ref in (own_ref, *refs[:-1]))
    refs[-1][...] = total.astype(BF16)


def input_body(residual, model, *refs):
    base, refs = (refs[0], refs[1:]) if residual else (None, refs)
    values_ref, factor_ref, dot_ref, own_ref, *came, out_ref = refs
    width = own_ref.shape[1]
    total = own_ref[...].astype(F32)
    dot_total = dot_ref[:, :1]
    for ref in came:
        total = total + ref[:, :width].astype(F32)
        column = ref[:, width:].astype(F32)
        dot_total = dot_total + (column[:, :1] + column[:, 1:2] + column[:, 2:3])
    factor = factor_ref[:, :1]
    grad = factor * total - values_ref[...].astype(F32) * (
        factor * factor * factor * dot_total / model
    )
    if residual:
        grad = grad + base[...].astype(F32)
    out_ref[...] = grad.astype(BF16)


def flipped_bits(value, count):
    out, left = 0, count
    while left > 1:
        out = out * 2 + value % 2
        value, left = value // 2, left // 2
    return out


def tokens_body(at_ref, left_ref, right_ref, keep_ref, *send_refs):
    both = dot(left_ref[...], right_ref[...], TN).astype(BF16)
    half = both.shape[0] // 2

    @pl.when(at_ref[0] == 0)
    def low():
        keep_ref[0] = both[:half]

    @pl.when(at_ref[0] == 1)
    def high():
        keep_ref[0] = both[half:]

    tall = send_refs[0].shape[0]
    place = pl.program_id(0)
    for group, send_ref in enumerate(send_refs):

        @pl.when((at_ref[0] == 0) & (place // tall == group))
        def low_sent(send_ref=send_ref):
            send_ref[place % tall] = both[half:]

        @pl.when((at_ref[0] == 1) & (place // tall == group))
        def high_sent(send_ref=send_ref):
            send_ref[place % tall] = both[:half]


def ordered(
    body, inputs, after, outs, grid, in_specs, out_specs, scalars, relay=(), scratch=()
):
    kept = 1 + len(inputs)
    first = kept + len(after)
    anywhere = pl.BlockSpec(memory_space=pl.ANY)

    def with_order(*refs):
        begin = first + len(relay)
        last = begin + len(outs)
        body(*refs[:kept], *refs[begin:last], *refs[last + len(relay) :])

    return pl.pallas_call(
        with_order,
        out_shape=outs + [struct(value.shape, value.dtype) for value in relay],
        grid_spec=pltpu.PrefetchScalarGridSpec(
            num_scalar_prefetch=1,
            grid=grid,
            in_specs=in_specs + [anywhere] * (len(after) + len(relay)),
            out_specs=out_specs + [anywhere] * len(relay),
            scratch_shapes=list(scratch),
        ),
        input_output_aliases={first + i: len(outs) + i for i in range(len(relay))},
        compiler_params=pltpu.CompilerParams(vmem_limit_bytes=16 * 1024 * 1024),
        cost_estimate=pl.CostEstimate(flops=0, bytes_accessed=1024, transcendentals=0),
    )(scalars, *inputs, *after, *relay)


def over_tokens(left, right, after=(), relay=(), natural=False):
    rows, model = left.shape
    chips = lax.axis_size("seq") // 2
    step = model // chips
    cols = right.shape[1]
    shard = lax.axis_index("seq").astype(jnp.int32)
    near = jnp.stack(
        [shard % 2]
        + [
            jnp.int32(i) if natural else lax.bitwise_xor(shard // 2, jnp.int32(flipped_bits(i, chips)))
            for i in range(chips)
        ]
    )
    share = (step // 2, cols)
    group = (chips // 2, *share)
    keep, low, high, *relayed = ordered(
        tokens_body,
        [left, right],
        after,
        [struct((chips, *share), BF16), struct(group, BF16), struct(group, BF16)],
        (chips,),
        [
            pl.BlockSpec((rows, step), lambda i, at: (0, at[1 + i])),
            pl.BlockSpec(right.shape, lambda i, at: (0, 0)),
        ],
        [pl.BlockSpec((1, *share), lambda i, at: (i, 0, 0))]
        + [pl.BlockSpec(group, lambda i, at: (0, 0, 0))] * 2,
        near,
        relay,
    )
    return keep, low, high, relayed


def add_body(at_ref, *refs):
    out_ref = refs[-1]
    for index in range(out_ref.shape[0]):
        total = sum(ref[index].astype(F32) for ref in refs[:-1])
        out_ref[index] = total.astype(out_ref.dtype)


def added(keep, came, terms, first, count, dtype, after, relay=()):
    rows, cols = keep.shape[1:]
    block = pl.BlockSpec((count, rows, cols), lambda i, at: (first // count, 0, 0))
    start = pl.BlockSpec((count, rows, cols), lambda i, at: (0, 0, 0))
    return ordered(
        add_body,
        [keep, came, *terms],
        after,
        [struct((count, rows, cols), dtype)],
        (1,),
        [block, start if came.shape[0] == count and first > 0 else block] + [block] * len(terms),
        [start],
        jnp.zeros((1,), jnp.int32),
        relay,
    )


def core_swap(value):
    count = lax.axis_size("seq")
    return lax.ppermute(value, "seq", [(shard, shard ^ 1) for shard in range(count)])


def whole_body(left_ref, right_ref, out_ref):
    out_ref[...] = dot(left_ref[...], right_ref[...], TN).astype(BF16)


def pieces_body(count, at_ref, *refs):
    pieces, (right_ref, out_ref) = refs[:count], refs[count:]
    for step, piece in enumerate(pieces):

        @pl.when(pl.program_id(0) == step)
        def multiply(piece=piece):
            out_ref[...] = dot(piece[...], right_ref[...], TN).astype(BF16)


def scattered(pieces, right, after=()):
    rows, width = pieces[0].shape
    count = len(pieces)
    block = width // 2 if count == 1 else width
    parts = width // block
    cols = right.shape[1]
    tp_id = lax.axis_index("tp").astype(jnp.int32)
    places = jnp.stack([lax.rem(tp_id + count - step, count) if count > 1 else tp_id * 0 for step in range(count)])

    def picked(which):
        def index(step, part, at):
            held = jnp.where(step < which, 0, parts - 1)
            return 0, jnp.where(step == which, part, held)

        return pl.BlockSpec((rows, block), index)

    (partial,) = ordered(
        functools.partial(pieces_body, count),
        [*pieces, right],
        after,
        [struct((width * count, cols), BF16)],
        (count, parts),
        [picked(which) for which in range(count)]
        + [pl.BlockSpec(right.shape, lambda step, part, at: (0, 0))],
        [pl.BlockSpec((block, cols), lambda step, part, at: (at[step] * parts + part, 0))],
        places,
    )
    return lax.psum_scatter(partial, "seq", scatter_dimension=0, tiled=True), partial


def chip_sum_body(count, keep_ref, *refs):
    came, refs = refs[:count], refs[count:]
    whole_ref, low_ref, high_ref, out_ref = *refs[:3], refs[3 + count]
    for index in range(count):
        total = keep_ref[index].astype(F32) + came[index][...].astype(F32)
        refs[3 + index][...] = total.astype(BF16)
    half = count // 2
    for index in range(count):
        other = low_ref[index] if index < half else high_ref[index - half]
        total = whole_ref[index].astype(F32) + other.astype(F32)
        out_ref[index] = total.astype(BF16)


def sums_below(keep, came, query, after):
    chips, rows, cols = keep.shape
    *sums, query_sum = call(
        functools.partial(chip_sum_body, chips),
        [struct((rows, cols), BF16)] * chips + [struct(query[0].shape, BF16)],
        [keep, *came, *query],
        0,
        2 * keep.size,
        after=after,
        limit=24,
    )
    terms = [sums[0]]
    for steps in range(1, chips):
        pairs = [(shard, shard - 2 * steps) for shard in range(2 * steps, 2 * chips)]
        terms.append(lax.ppermute(sums[steps], "seq", pairs))
    return terms, sums[0], query_sum


class Halving:
    def __init__(self, keep, low, high):
        self.keep = keep
        self.high, self.low = core_swap(high), core_swap(low)
        self.terms = []
        self.count = keep.shape[0]
        self.distance = 2

    def step(self, after, relay=()):
        self.count //= 2
        came = self.low if self.terms else self.high
        sent, *relayed = added(
            self.keep, came, self.terms, self.count, self.count, BF16, after, relay
        )
        pairs = [(shard, shard ^ self.distance) for shard in range(lax.axis_size("seq"))]
        self.terms.append(lax.ppermute(sent, "seq", pairs))
        self.distance *= 2
        return sent, relayed

    def finish(self, after):
        rows, cols = self.keep.shape[1:]
        sections = lax.axis_size("section")
        section = lax.axis_index("section")
        share = rows // sections
        piece = struct((share, cols), BF16)
        block = pl.BlockSpec((2, rows, cols), lambda i, at: (0, 0, 0))
        flat = pl.BlockSpec((share, cols), lambda i, at: (0, 0))
        targets = [lax.rem(section + step, sections) for step in range(sections)]
        outs = ordered(
            last_body,
            [self.keep, self.low, *self.terms],
            after,
            [piece] * (2 * sections),
            (1,),
            [block] * (2 + len(self.terms)),
            [flat] * (2 * sections),
            jnp.stack(targets).astype(jnp.int32),
            scratch=[pltpu.VMEM((2, rows, cols), F32)],
        )
        count = lax.axis_size("seq")
        parts = list(outs[:1])
        for step in range(sections):
            pairs = [
                (shard * sections + one, (shard ^ self.distance) * sections + (one + step) % sections)
                for shard in range(count)
                for one in range(sections)
            ]
            parts.append(lax.ppermute(outs[sections + step], ("seq", "section"), pairs))
            if step > 0:
                parts.append(shifted(outs[step], "section", step))
        return parts


def last_body(at_ref, *refs):
    sections = at_ref.shape[0]
    terms, outs, total_ref = refs[: -2 * sections - 1], refs[-2 * sections - 1 : -1], refs[-1]
    share = outs[0].shape[0]
    for place in range(2):
        total_ref[place] = sum(ref[place].astype(F32) for ref in terms)
        for step in range(sections):
            span = pl.ds(pl.multiple_of(at_ref[step] * share, share), share)
            outs[place * sections + step][...] = total_ref[place, span, :].astype(BF16)


def section_body(sections, section_ref, *refs):
    parts, (self_ref, cache_ref) = refs[:-2], refs[-2:]
    section = section_ref[0]
    groups = [[parts[0], parts[1]]] + [
        [parts[2 * step], parts[2 * step + 1]] for step in range(1, sections)
    ]
    own = jnp.zeros(parts[0].shape, F32)
    other = jnp.zeros(parts[0].shape, F32)
    for step, group in enumerate(groups):
        total = group[0][...].astype(F32) + group[1][...].astype(F32)
        from_self = jnp.full(total.shape, section, jnp.int32) == step
        own = own + jnp.where(from_self, total, 0.0)
        other = other + jnp.where(from_self, 0.0, total)
    half = own.shape[1] // 2
    for kind in range(2):
        self_ref[:, kind, :] = own[:, kind * half : (kind + 1) * half]
        cache_ref[:, kind, :] = other[:, kind * half : (kind + 1) * half]


def flip_body(value_ref, out_ref):
    out_ref[...] = value_ref[...].astype(F32).T


def same_body(value_ref, out_ref):
    out_ref[...] = value_ref[...]


def wide_body(value_ref, out_ref):
    out_ref[...] = value_ref[...].astype(F32)


def on_device(
    h_in,
    memory,
    cotangent,
    block_docs,
    w_query,
    w_out,
    self_key_value_weight,
    cache_key_value_weight,
):
    section_id = lax.axis_index("section")
    section_count = lax.axis_size("section")
    shard_id = lax.axis_index("seq")
    tp_id = lax.axis_index("tp")
    tp_count = lax.axis_size("tp")
    self_section = section_id == 0
    hidden = h_in[0]
    grad_local = cotangent[0]
    source = jnp.where(self_section, hidden, memory[0])

    def gathered(own):
        return [own] + [shifted(own, "tp", step) for step in range(1, tp_count)]

    source_pieces = gathered(source)
    hidden_pieces = gathered(hidden)
    grad_pieces = gathered(grad_local)

    rows, width = hidden.shape
    model = width * tp_count
    per = rows // BLK
    query_weight = w_query[0]
    out_weight = w_out[0]
    kv_weight = jnp.where(self_section, self_key_value_weight, cache_key_value_weight)
    kv_cols = self_key_value_weight.shape[2]
    kv_heads = kv_cols // HEAD_DIM
    query_cols = query_weight.shape[1]
    heads = query_cols // HEAD_DIM
    kv_flat = kv_weight.reshape(model, 2 * kv_cols)
    me = tp_id.astype(jnp.int32).reshape(1)

    all_docs = lax.all_gather(block_docs[0], "seq", axis=0, tiled=True)
    first_doc = lax.dynamic_slice_in_dim(all_docs, shard_id * per, 1)[0]
    first_block = jnp.sum((all_docs < first_doc).astype(jnp.int32)) // per
    window_block = jnp.maximum(shard_id * rows - WIN + 1, 0) // rows
    first_block = jnp.where(self_section, jnp.maximum(first_block, window_block), first_block)
    meta = jnp.concatenate(
        [
            jnp.stack([shard_id, self_section.astype(jnp.int32), first_block]).astype(jnp.int32),
            all_docs,
        ]
    )

    source_normed, source_factor, packed, key_raw = call(
        functools.partial(key_body, tp_count),
        [
            struct((rows, model), BF16),
            struct((rows, HEAD_DIM), F32),
            struct((rows, 2 * kv_cols), BF16),
            struct((rows, kv_cols), F32),
        ],
        [me, *source_pieces, kv_flat],
        1,
        2 * rows * model * 2 * kv_cols,
        limit=40,
        after=[meta],
    )
    all_kv = lax.all_gather(packed, "seq", axis=0, tiled=True)
    length = all_kv.shape[0]
    chips = length // rows // 2

    together = 2 if heads % 2 == 0 else 1
    whole = pl.BlockSpec((rows, width), lambda i: (0, 0))
    full = pl.BlockSpec((rows, model), lambda i: (0, 0))
    per_head = pl.BlockSpec((together, rows, HEAD_DIM), lambda i: (i, 0, 0))
    normed, row_factor, query_unit, query_raw = call(
        functools.partial(query_body, tp_count),
        [
            struct((rows, model), BF16),
            struct((rows, HEAD_DIM), F32),
            struct((heads, rows, HEAD_DIM), BF16),
            struct((heads, rows, HEAD_DIM), F32),
        ],
        [me, *hidden_pieces, query_weight],
        1,
        2 * rows * model * query_cols,
        after=[packed],
        grid=(heads // together,),
        in_specs=[SMEM]
        + [whole] * tp_count
        + [pl.BlockSpec((model, together * HEAD_DIM), lambda i: (0, i))],
        out_specs=[
            full,
            pl.BlockSpec((rows, HEAD_DIM), lambda i: (0, 0)),
            per_head,
            per_head,
        ],
    )
    attn_flat, log_denom = call(
        functools.partial(forward_body, kv_heads),
        [struct((rows, query_cols), BF16), struct((heads, rows, HEAD_DIM), F32)],
        [meta, query_unit, all_kv],
        1,
        4 * rows * length * query_cols,
        [pltpu.VMEM((heads, rows, HEAD_DIM), F32)] * 2,
    )
    out_share, mark = scattered(grad_pieces, attn_flat)
    (grad_attn,) = call(
        functools.partial(grad_attn_body, tp_count),
        [struct((heads, rows, HEAD_DIM), BF16)],
        [me, *grad_pieces, out_weight],
        1,
        2 * rows * model * query_cols,
        after=[mark],
        grid=(heads // together,),
        in_specs=[SMEM]
        + [whole] * tp_count
        + [pl.BlockSpec((together * HEAD_DIM, model), lambda i: (i, 0))],
        out_specs=[per_head],
    )
    halves = [struct((chips, rows, 2 * kv_cols), BF16)] + [
        struct((rows, 2 * kv_cols), BF16)
    ] * chips
    keep, *send, grad_queries = call(
        functools.partial(backward_body, kv_heads),
        halves + [struct((rows, query_cols), BF16)],
        [meta, query_unit, query_raw, grad_attn, attn_flat, log_denom, all_kv],
        1,
        10 * rows * length * query_cols,
        [pltpu.VMEM((heads, rows, HEAD_DIM), F32)] * 2,
        after=[mark],
    )
    kv_came = [core_swap(piece) for piece in send]
    query_keep, query_low, query_high, _ = over_tokens(normed, grad_queries, natural=True)
    kv_sums, mark, query_sum = sums_below(
        keep, kv_came, [query_keep, core_swap(query_low), core_swap(query_high)], []
    )
    query_share = lax.psum_scatter(
        query_sum.reshape(-1, query_cols),
        "seq",
        scatter_dimension=0,
        tiled=True,
        axis_index_groups=[[2 * one + core for one in range(chips)] for core in range(2)],
    )

    wide = struct((rows, width), BF16)
    broad = struct((rows, HEAD_DIM), F32)
    projected, *projected_sent = call(
        functools.partial(project_body, tp_count),
        split_shapes(rows, width, tp_count, False),
        [me, attn_flat, out_weight],
        1,
        2 * rows * model * query_cols,
        after=[mark],
    )
    rows_part, *rows_sent, row_dot = call(
        functools.partial(back_body, tp_count),
        split_shapes(rows, width, tp_count, True) + [broad],
        [me, grad_queries, query_weight, *hidden_pieces],
        1,
        2 * rows * model * query_cols,
        after=[projected],
    )
    (kv_grad,) = call(
        key_grad_body,
        [struct((rows, 2 * kv_cols), BF16)],
        [key_raw, *kv_sums],
        0,
        0,
        after=[row_dot],
        limit=16,
    )
    kv_keep, kv_low, kv_high, relayed = over_tokens(
        source_normed, kv_grad, (), [*rows_sent, *projected_sent]
    )
    others = tp_count - 1
    projected_came = sent_over_tp(relayed[others:])
    rows_came = sent_over_tp(relayed[:others])
    kv_sum = Halving(kv_keep, kv_low, kv_high)
    source_part, *source_sent, source_dot = call(
        functools.partial(back_body, tp_count),
        split_shapes(rows, width, tp_count, True) + [broad],
        [me, kv_grad, kv_flat, *source_pieces],
        1,
        4 * rows * model * kv_cols,
        after=[kv_keep],
    )
    mark, source_sent = kv_sum.step([source_dot], source_sent)
    source_came = sent_over_tp(source_sent)
    (h_out,) = call(output_body, [wide], [hidden, projected, *projected_came], 0, 0, after=[mark])
    passed_came = shifted(h_out, "section", 1)
    mark = h_out
    while kv_sum.count > 2:
        mark, _ = kv_sum.step([mark])
    kv_parts = kv_sum.finish([mark])
    (grad_input,) = call(
        functools.partial(input_body, True, model),
        [wide],
        [grad_local, hidden, row_factor, row_dot, rows_part, *rows_came],
        0,
        0,
        after=[kv_parts[0]],
    )
    (grad_memory,) = call(
        functools.partial(input_body, False, model),
        [wide],
        [source, source_factor, source_dot, source_part, *source_came],
        0,
        0,
        after=[grad_input],
    )
    (passed,) = call(same_body, [wide], [passed_came], 0, 0, after=[grad_memory])
    (out_grad,) = call(
        flip_body,
        [struct((query_cols, out_share.shape[0]), F32)],
        [out_share],
        0,
        0,
        after=[passed],
    )
    (query_grad,) = call(
        wide_body, [struct(query_share.shape, F32)], [query_share], 0, 0, after=[out_grad]
    )
    share_rows = kv_parts[0].shape[0]
    self_grad, cache_grad = call(
        functools.partial(section_body, section_count),
        [struct((share_rows, 2, kv_cols), F32)] * 2,
        [section_id.astype(jnp.int32).reshape(1), *kv_parts],
        1,
        0,
        after=[query_grad],
    )
    return (
        passed[None],
        grad_input[None],
        grad_memory[None],
        query_grad[None],
        out_grad[None],
        self_grad,
        cache_grad,
    )


def solution(mesh):
    return jax.shard_map(
        on_device,
        mesh=mesh,
        in_specs=(
            P("section", "seq", "tp"),
            P("section", "seq", "tp"),
            P("section", "seq", "tp"),
            P("section", "seq"),
            P("section", None, "tp"),
            P("section", "tp", None),
            P(None, None, "tp"),
            P(None, None, "tp"),
        ),
        out_specs=(
            P("section", "seq", "tp"),
            P("section", "seq", "tp"),
            P("section", "seq", "tp"),
            P("section", "seq", "tp"),
            P("section", "tp", "seq"),
            P(("seq", "section"), None, "tp"),
            P(("seq", "section"), None, "tp"),
        ),
        check_vma=False,
    )
```

```python
import functools
import math

import jax
import jax.numpy as jnp
from jax import lax
from jax.experimental import pallas as pl
from jax.experimental.pallas import tpu as pltpu
from jax.sharding import PartitionSpec as P

HEAD_DIM = 128
BLK = 128
WIN = 1024

score_scale = 40.0
norm_eps = 1e-06
log2_e = math.log2(math.e)

F32 = jnp.float32
BF16 = jnp.bfloat16
NN = (((1,), (0,)), ((), ()))
NT = (((1,), (1,)), ((), ()))
TN = (((0,), (0,)), ((), ()))

VMEM = pl.BlockSpec(memory_space=pltpu.VMEM)
SMEM = pl.BlockSpec(memory_space=pltpu.SMEM)


def dot(left, right, dims):
    return lax.dot_general(left, right, dims, preferred_element_type=F32)


def shifted(value, axis, steps):
    count = lax.axis_size(axis)
    pairs = [(source, (source + steps) % count) for source in range(count)]
    return lax.ppermute(value, axis, pairs)


def call(
    body, out_shape, inputs, smem_count, flops, scratch=(), limit=60, after=(),
    grid=(), in_specs=None, out_specs=None,
):
    moved = sum(v.size * v.dtype.itemsize for v in inputs) + sum(
        o.size * o.dtype.itemsize for o in out_shape
    )
    if in_specs is None:
        in_specs = [SMEM] * smem_count + [VMEM] * (len(inputs) - smem_count)
    if out_specs is None:
        out_specs = [VMEM] * len(out_shape)

    def with_order(*refs):
        body(*refs[: len(inputs)], *refs[len(inputs) + len(after) :])

    return pl.pallas_call(
        with_order,
        out_shape=out_shape,
        grid=grid,
        in_specs=list(in_specs) + [pl.BlockSpec(memory_space=pl.ANY)] * len(after),
        out_specs=out_specs,
        scratch_shapes=list(scratch),
        compiler_params=pltpu.CompilerParams(vmem_limit_bytes=limit * 1024 * 1024),
        cost_estimate=pl.CostEstimate(flops=flops, bytes_accessed=moved, transcendentals=0),
    )(*inputs, *after)


def struct(shape, dtype):
    return jax.ShapeDtypeStruct(shape, dtype)


def offset(me, count, step, width):
    return pl.multiple_of(lax.rem(me + count - step, count) * width, width)


def normalize(pieces, me, normed_ref, factor_ref):
    count = len(pieces)
    width = pieces[0].shape[1]
    total = 0.0
    for piece in pieces:
        wide = piece[...].astype(F32)
        total = total + jnp.sum(wide * wide, axis=1, keepdims=True)
    factor = lax.rsqrt(total / (count * width) + norm_eps)
    factor_ref[...] = jnp.broadcast_to(factor, factor_ref.shape)
    for step, piece in enumerate(pieces):
        normed_ref[:, pl.ds(offset(me, count, step, width), width)] = (
            piece[...].astype(F32) * factor
        ).astype(BF16)


def unit(raw):
    return raw * lax.rsqrt(jnp.sum(raw * raw, axis=1, keepdims=True) + norm_eps)


def unit_back(raw, grad):
    scale = lax.rsqrt(jnp.sum(raw * raw, axis=1, keepdims=True) + norm_eps)
    along = jnp.sum(raw * grad, axis=1, keepdims=True)
    return scale * grad - raw * (scale * scale * scale * along)


def query_body(count, me_ref, *refs):
    pieces, (weight, normed_ref, factor_ref, unit_ref, raw_ref) = refs[:count], refs[count:]

    @pl.when(pl.program_id(0) == 0)
    def first():
        normalize(pieces, me_ref[0], normed_ref, factor_ref)

    both = dot(normed_ref[...], weight[...], NN)
    for head in range(unit_ref.shape[0]):
        raw = both[:, head * HEAD_DIM : (head + 1) * HEAD_DIM]
        raw_ref[head] = raw
        unit_ref[head] = unit(raw).astype(BF16)


def key_body(count, me_ref, *refs):
    pieces, (weight, normed_ref, factor_ref, packed_ref, raw_ref) = refs[:count], refs[count:]
    normalize(pieces, me_ref[0], normed_ref, factor_ref)
    both = dot(normed_ref[...], weight[...], NN)
    half = both.shape[1] // 2
    for head in range(half // HEAD_DIM):
        cols = slice(head * HEAD_DIM, (head + 1) * HEAD_DIM)
        packed_ref[:, cols] = unit(both[:, cols]).astype(BF16)
    packed_ref[:, half:] = both[:, half:].astype(BF16)
    raw_ref[...] = both[:, :half]


def allowed_block(meta, block, rows):
    per = rows // BLK
    shard, self_section = meta[0], meta[1]
    shape = (rows, rows)
    query = lax.broadcasted_iota(jnp.int32, shape, 0)
    key = lax.broadcasted_iota(jnp.int32, shape, 1)
    query_doc = jnp.full(shape, meta[3 + shard * per], jnp.int32)
    key_doc = jnp.full(shape, meta[3 + block * per], jnp.int32)
    for part in range(1, per):
        query_doc = jnp.where(query >= part * BLK, meta[3 + shard * per + part], query_doc)
        key_doc = jnp.where(key >= part * BLK, meta[3 + block * per + part], key_doc)
    query_pos = shard * rows + query
    key_pos = block * rows + key
    is_self = jnp.full(shape, self_section, jnp.int32) == 1
    upper = jnp.where(is_self, query_pos, query_pos // BLK * BLK + BLK - 1)
    lower = jnp.where(is_self, query_pos - WIN, -1)
    return (query_doc == key_doc) & (key_pos <= upper) & (key_pos > lower)


def key_value(kv_ref, span, kv_head, kv_heads):
    first = (kv_heads + kv_head) * HEAD_DIM
    key = kv_ref[span, kv_head * HEAD_DIM : (kv_head + 1) * HEAD_DIM]
    return key, kv_ref[span, first : first + HEAD_DIM]


def forward_body(kv_heads, meta, query_ref, kv_ref, out_ref, log_ref, number_ref, denom_ref):
    heads, rows, _ = query_ref.shape
    group = heads // kv_heads
    stacked = (group * rows, HEAD_DIM)
    number_ref[...] = jnp.zeros_like(number_ref)
    denom_ref[...] = jnp.zeros_like(denom_ref)

    def step(block, carry):
        allowed = allowed_block(meta, block, rows)
        span = pl.ds(pl.multiple_of(block * rows, rows), rows)
        for kv_head in range(kv_heads):
            mine = slice(kv_head * group, (kv_head + 1) * group)
            key, value = key_value(kv_ref, span, kv_head, kv_heads)
            score = dot(query_ref[mine].reshape(stacked), key, NT).reshape(group, rows, rows)
            weight = jnp.where(allowed[None], jnp.exp2(score * (score_scale * log2_e)), 0.0)
            folded = weight[:, :, :HEAD_DIM]
            for first in range(HEAD_DIM, rows, HEAD_DIM):
                folded = folded + weight[:, :, first : first + HEAD_DIM]
            denom_ref[mine] += folded
            product = dot(weight.astype(BF16).reshape(group * rows, rows), value, NN)
            number_ref[mine] += product.reshape(group, rows, HEAD_DIM)
        return carry

    lax.fori_loop(meta[2], meta[0] + 1, step, 0)
    for head in range(heads):
        denom = jnp.sum(denom_ref[head], axis=1, keepdims=True)
        log_ref[head] = jnp.broadcast_to(jnp.log2(denom), (rows, HEAD_DIM))
        out_ref[:, head * HEAD_DIM : (head + 1) * HEAD_DIM] = (number_ref[head] / denom).astype(BF16)


def grad_attn_body(count, me_ref, *refs):
    pieces, (weight, grad_ref) = refs[:count], refs[count:]
    width = pieces[0].shape[1]
    both = 0.0
    for step, piece in enumerate(pieces):
        span = pl.ds(offset(me_ref[0], count, step, width), width)
        both = both + dot(piece[...], weight[:, span], NT)
    for head in range(grad_ref.shape[0]):
        grad_ref[head] = both[:, head * HEAD_DIM : (head + 1) * HEAD_DIM].astype(BF16)


def backward_body(
    kv_heads, meta, query_ref, raw_ref, grad_ref, out_ref, log_ref, kv_ref,
    keep_ref, *refs,
):
    *send_refs, queries_ref, running_ref, delta_ref = refs
    heads, rows, _ = query_ref.shape
    group = heads // kv_heads
    stacked = (group * rows, HEAD_DIM)
    running_ref[...] = jnp.zeros_like(running_ref)
    keep_ref[...] = jnp.zeros_like(keep_ref)
    for send_ref in send_refs:
        send_ref[...] = jnp.zeros_like(send_ref)
    for head in range(heads):
        cols = slice(head * HEAD_DIM, (head + 1) * HEAD_DIM)
        product = grad_ref[head].astype(F32) * out_ref[:, cols].astype(F32)
        delta_ref[head] = jnp.broadcast_to(jnp.sum(product, axis=1, keepdims=True), (rows, HEAD_DIM))

    def widened(ref, mine):
        return jnp.concatenate([ref[mine].reshape(stacked)] * (rows // HEAD_DIM), axis=1)

    def step(block, carry):
        allowed = allowed_block(meta, block, rows)
        span = pl.ds(pl.multiple_of(block * rows, rows), rows)
        for kv_head in range(kv_heads):
            mine = slice(kv_head * group, (kv_head + 1) * group)
            key, value = key_value(kv_ref, span, kv_head, kv_heads)
            query = query_ref[mine].reshape(stacked)
            grad = grad_ref[mine].reshape(stacked)
            score = dot(query, key, NT)
            probs = jnp.exp2(score * (score_scale * log2_e) - widened(log_ref, mine))
            probs = jnp.where(allowed[None], probs.reshape(group, rows, rows), 0.0)
            probs = probs.reshape(group * rows, rows)
            grad_probs = dot(grad, value, NT)
            grad_scores = (probs * (grad_probs - widened(delta_ref, mine))).astype(BF16)
            running_ref[mine] += dot(grad_scores, key, NN).reshape(group, rows, HEAD_DIM)
            key_term = (score_scale * dot(grad_scores, query, TN)).astype(BF16)
            value_term = dot(probs.astype(BF16), grad, TN).astype(BF16)
            low = kv_head * HEAD_DIM
            high = (kv_heads + kv_head) * HEAD_DIM

            steps = meta[0] // 2 - block // 2
            same_core = block % 2 == meta[0] % 2

            @pl.when(same_core)
            def own():
                keep_ref[steps, :, low : low + HEAD_DIM] = key_term
                keep_ref[steps, :, high : high + HEAD_DIM] = value_term

            for place, send_ref in enumerate(send_refs):

                def other(send_ref=send_ref):
                    send_ref[:, low : low + HEAD_DIM] = key_term
                    send_ref[:, high : high + HEAD_DIM] = value_term

                pl.when(jnp.logical_not(same_core) & (steps == place))(other)
        return carry

    lax.fori_loop(meta[2], meta[0] + 1, step, 0)
    for head in range(heads):
        queries_ref[:, head * HEAD_DIM : (head + 1) * HEAD_DIM] = unit_back(
            raw_ref[head], score_scale * running_ref[head]
        ).astype(BF16)


def split(count, transposed, me, left, weight_ref, pieces, outs, dot_ref):
    rows, width = outs[0].shape
    total = 0.0
    for step in list(range(1, count)) + [0]:
        span = pl.ds(offset(me, count, step, width), width)
        if transposed:
            part = dot(left, weight_ref[span, :], NT).astype(BF16)
        else:
            part = dot(left, weight_ref[:, span], NN).astype(BF16)
        outs[step][:, :width] = part
        if dot_ref is not None:
            total = total + jnp.sum(
                part.astype(F32) * pieces[step][...].astype(F32), axis=1, keepdims=True
            )
    if dot_ref is not None:
        dot_ref[...] = jnp.broadcast_to(total, dot_ref.shape)
        lane = lax.broadcasted_iota(jnp.int32, dot_ref.shape, 1)
        rest, column = total, jnp.zeros(dot_ref.shape, F32)
        for place in range(3):
            term = rest.astype(BF16).astype(F32)
            column = jnp.where(lane == place, term, column)
            rest = rest - term
        for out in outs[1:]:
            out[:, width:] = column.astype(BF16)


def split_shapes(rows, width, count, dotted):
    extra = HEAD_DIM if dotted else 0
    return [struct((rows, width), BF16)] + [struct((rows, width + extra), BF16)] * (count - 1)


def sent_over_tp(outs):
    return [shifted(out, "tp", -1 - index) for index, out in enumerate(outs)]


def project_body(count, me_ref, left_ref, weight_ref, *outs):
    split(count, False, me_ref[0], left_ref[...], weight_ref, None, outs, None)


def back_body(count, me_ref, left_ref, weight_ref, *refs):
    pieces, outs, dot_ref = refs[:count], refs[count:-1], refs[-1]
    split(count, True, me_ref[0], left_ref[...], weight_ref, pieces, outs, dot_ref)


def key_grad_body(raw_ref, *refs):
    term_refs, grad_ref = refs[:-1], refs[-1]
    half = raw_ref.shape[1]
    total = sum(term[...].astype(F32) for term in term_refs)
    for first in range(0, half, HEAD_DIM):
        cols = slice(first, first + HEAD_DIM)
        grad_ref[:, cols] = unit_back(raw_ref[:, cols], total[:, cols]).astype(BF16)
    grad_ref[:, half:] = total[:, half:].astype(BF16)


def output_body(at_ref, hidden_ref, own_ref, *refs):
    total = hidden_ref[...].astype(F32) + sum(ref[...].astype(F32) for ref in (own_ref, *refs[:-1]))
    refs[-1][...] = total.astype(BF16)


def input_body(residual, model, *refs):
    base, refs = (refs[0], refs[1:]) if residual else (None, refs)
    values_ref, factor_ref, dot_ref, own_ref, *came, out_ref = refs
    width = own_ref.shape[1]
    total = own_ref[...].astype(F32)
    dot_total = dot_ref[:, :1]
    for ref in came:
        total = total + ref[:, :width].astype(F32)
        column = ref[:, width:].astype(F32)
        dot_total = dot_total + (column[:, :1] + column[:, 1:2] + column[:, 2:3])
    factor = factor_ref[:, :1]
    grad = factor * total - values_ref[...].astype(F32) * (
        factor * factor * factor * dot_total / model
    )
    if residual:
        grad = grad + base[...].astype(F32)
    out_ref[...] = grad.astype(BF16)


def flipped_bits(value, count):
    out, left = 0, count
    while left > 1:
        out = out * 2 + value % 2
        value, left = value // 2, left // 2
    return out


def tokens_body(at_ref, left_ref, right_ref, keep_ref, *send_refs):
    both = dot(left_ref[...], right_ref[...], TN).astype(BF16)
    half = both.shape[0] // 2

    @pl.when(at_ref[0] == 0)
    def low():
        keep_ref[0] = both[:half]

    @pl.when(at_ref[0] == 1)
    def high():
        keep_ref[0] = both[half:]

    tall = send_refs[0].shape[0]
    place = pl.program_id(0)
    for group, send_ref in enumerate(send_refs):

        @pl.when((at_ref[0] == 0) & (place // tall == group))
        def low_sent(send_ref=send_ref):
            send_ref[place % tall] = both[half:]

        @pl.when((at_ref[0] == 1) & (place // tall == group))
        def high_sent(send_ref=send_ref):
            send_ref[place % tall] = both[:half]


def ordered(
    body, inputs, after, outs, grid, in_specs, out_specs, scalars, relay=(), scratch=()
):
    kept = 1 + len(inputs)
    first = kept + len(after)
    anywhere = pl.BlockSpec(memory_space=pl.ANY)

    def with_order(*refs):
        begin = first + len(relay)
        last = begin + len(outs)
        body(*refs[:kept], *refs[begin:last], *refs[last + len(relay) :])

    return pl.pallas_call(
        with_order,
        out_shape=outs + [struct(value.shape, value.dtype) for value in relay],
        grid_spec=pltpu.PrefetchScalarGridSpec(
            num_scalar_prefetch=1,
            grid=grid,
            in_specs=in_specs + [anywhere] * (len(after) + len(relay)),
            out_specs=out_specs + [anywhere] * len(relay),
            scratch_shapes=list(scratch),
        ),
        input_output_aliases={first + i: len(outs) + i for i in range(len(relay))},
        compiler_params=pltpu.CompilerParams(vmem_limit_bytes=16 * 1024 * 1024),
        cost_estimate=pl.CostEstimate(flops=0, bytes_accessed=1024, transcendentals=0),
    )(scalars, *inputs, *after, *relay)


def over_tokens(left, right, after=(), relay=(), natural=False):
    rows, model = left.shape
    chips = lax.axis_size("seq") // 2
    step = model // chips
    cols = right.shape[1]
    shard = lax.axis_index("seq").astype(jnp.int32)
    near = jnp.stack(
        [shard % 2]
        + [
            jnp.int32(i) if natural else lax.bitwise_xor(shard // 2, jnp.int32(flipped_bits(i, chips)))
            for i in range(chips)
        ]
    )
    share = (step // 2, cols)
    group = (chips // 2, *share)
    keep, low, high, *relayed = ordered(
        tokens_body,
        [left, right],
        after,
        [struct((chips, *share), BF16), struct(group, BF16), struct(group, BF16)],
        (chips,),
        [
            pl.BlockSpec((rows, step), lambda i, at: (0, at[1 + i])),
            pl.BlockSpec(right.shape, lambda i, at: (0, 0)),
        ],
        [pl.BlockSpec((1, *share), lambda i, at: (i, 0, 0))]
        + [pl.BlockSpec(group, lambda i, at: (0, 0, 0))] * 2,
        near,
        relay,
    )
    return keep, low, high, relayed


def add_body(at_ref, *refs):
    out_ref = refs[-1]
    for index in range(out_ref.shape[0]):
        total = sum(ref[index].astype(F32) for ref in refs[:-1])
        out_ref[index] = total.astype(out_ref.dtype)


def added(keep, came, terms, first, count, dtype, after, relay=()):
    rows, cols = keep.shape[1:]
    block = pl.BlockSpec((count, rows, cols), lambda i, at: (first // count, 0, 0))
    start = pl.BlockSpec((count, rows, cols), lambda i, at: (0, 0, 0))
    return ordered(
        add_body,
        [keep, came, *terms],
        after,
        [struct((count, rows, cols), dtype)],
        (1,),
        [block, start if came.shape[0] == count and first > 0 else block] + [block] * len(terms),
        [start],
        jnp.zeros((1,), jnp.int32),
        relay,
    )


def core_swap(value):
    count = lax.axis_size("seq")
    return lax.ppermute(value, "seq", [(shard, shard ^ 1) for shard in range(count)])


def whole_body(left_ref, right_ref, out_ref):
    out_ref[...] = dot(left_ref[...], right_ref[...], TN).astype(BF16)


def pieces_body(count, at_ref, *refs):
    pieces, (right_ref, out_ref) = refs[:count], refs[count:]
    for step, piece in enumerate(pieces):

        @pl.when(pl.program_id(0) == step)
        def multiply(piece=piece):
            out_ref[...] = dot(piece[...], right_ref[...], TN).astype(BF16)


def scattered(pieces, right, after=()):
    rows, width = pieces[0].shape
    count = len(pieces)
    block = width // 2 if count == 1 else width
    parts = width // block
    cols = right.shape[1]
    tp_id = lax.axis_index("tp").astype(jnp.int32)
    places = jnp.stack([lax.rem(tp_id + count - step, count) if count > 1 else tp_id * 0 for step in range(count)])

    def picked(which):
        def index(step, part, at):
            held = jnp.where(step < which, 0, parts - 1)
            return 0, jnp.where(step == which, part, held)

        return pl.BlockSpec((rows, block), index)

    (partial,) = ordered(
        functools.partial(pieces_body, count),
        [*pieces, right],
        after,
        [struct((width * count, cols), BF16)],
        (count, parts),
        [picked(which) for which in range(count)]
        + [pl.BlockSpec(right.shape, lambda step, part, at: (0, 0))],
        [pl.BlockSpec((block, cols), lambda step, part, at: (at[step] * parts + part, 0))],
        places,
    )
    return lax.psum_scatter(partial, "seq", scatter_dimension=0, tiled=True), partial


def chip_sum_body(count, keep_ref, *refs):
    came, refs = refs[:count], refs[count:]
    whole_ref, low_ref, high_ref, out_ref = *refs[:3], refs[3 + count]
    for index in range(count):
        total = keep_ref[index].astype(F32) + came[index][...].astype(F32)
        refs[3 + index][...] = total.astype(BF16)
    half = count // 2
    for index in range(count):
        other = low_ref[index] if index < half else high_ref[index - half]
        total = whole_ref[index].astype(F32) + other.astype(F32)
        out_ref[index] = total.astype(BF16)


def sums_below(keep, came, query, after):
    chips, rows, cols = keep.shape
    *sums, query_sum = call(
        functools.partial(chip_sum_body, chips),
        [struct((rows, cols), BF16)] * chips + [struct(query[0].shape, BF16)],
        [keep, *came, *query],
        0,
        2 * keep.size,
        after=after,
        limit=24,
    )
    terms = [sums[0]]
    for steps in range(1, chips):
        pairs = [(shard, shard - 2 * steps) for shard in range(2 * steps, 2 * chips)]
        terms.append(lax.ppermute(sums[steps], "seq", pairs))
    return terms, sums[0], query_sum


class Halving:
    def __init__(self, keep, low, high):
        self.keep = keep
        self.high, self.low = core_swap(high), core_swap(low)
        self.terms = []
        self.count = keep.shape[0]
        self.distance = 2

    def step(self, after, relay=()):
        self.count //= 2
        came = self.low if self.terms else self.high
        sent, *relayed = added(
            self.keep, came, self.terms, self.count, self.count, BF16, after, relay
        )
        pairs = [(shard, shard ^ self.distance) for shard in range(lax.axis_size("seq"))]
        self.terms.append(lax.ppermute(sent, "seq", pairs))
        self.distance *= 2
        return sent, relayed

    def finish(self, after):
        rows, cols = self.keep.shape[1:]
        sections = lax.axis_size("section")
        section = lax.axis_index("section")
        share = rows // sections
        piece = struct((share, cols), BF16)
        block = pl.BlockSpec((2, rows, cols), lambda i, at: (0, 0, 0))
        flat = pl.BlockSpec((share, cols), lambda i, at: (0, 0))
        targets = [lax.rem(section + step, sections) for step in range(sections)]
        outs = ordered(
            last_body,
            [self.keep, self.low, *self.terms],
            after,
            [piece] * (2 * sections),
            (1,),
            [block] * (2 + len(self.terms)),
            [flat] * (2 * sections),
            jnp.stack(targets).astype(jnp.int32),
            scratch=[pltpu.VMEM((2, rows, cols), F32)],
        )
        count = lax.axis_size("seq")
        parts = list(outs[:1])
        for step in range(sections):
            pairs = [
                (shard * sections + one, (shard ^ self.distance) * sections + (one + step) % sections)
                for shard in range(count)
                for one in range(sections)
            ]
            parts.append(lax.ppermute(outs[sections + step], ("seq", "section"), pairs))
            if step > 0:
                parts.append(shifted(outs[step], "section", step))
        return parts


def last_body(at_ref, *refs):
    sections = at_ref.shape[0]
    terms, outs, total_ref = refs[: -2 * sections - 1], refs[-2 * sections - 1 : -1], refs[-1]
    share = outs[0].shape[0]
    for place in range(2):
        total_ref[place] = sum(ref[place].astype(F32) for ref in terms)
        for step in range(sections):
            span = pl.ds(pl.multiple_of(at_ref[step] * share, share), share)
            outs[place * sections + step][...] = total_ref[place, span, :].astype(BF16)


def section_body(sections, section_ref, *refs):
    parts, (self_ref, cache_ref) = refs[:-2], refs[-2:]
    section = section_ref[0]
    groups = [[parts[0], parts[1]]] + [
        [parts[2 * step], parts[2 * step + 1]] for step in range(1, sections)
    ]
    own = jnp.zeros(parts[0].shape, F32)
    other = jnp.zeros(parts[0].shape, F32)
    for step, group in enumerate(groups):
        total = group[0][...].astype(F32) + group[1][...].astype(F32)
        from_self = jnp.full(total.shape, section, jnp.int32) == step
        own = own + jnp.where(from_self, total, 0.0)
        other = other + jnp.where(from_self, 0.0, total)
    half = own.shape[1] // 2
    for kind in range(2):
        self_ref[:, kind, :] = own[:, kind * half : (kind + 1) * half]
        cache_ref[:, kind, :] = other[:, kind * half : (kind + 1) * half]


def flip_body(value_ref, out_ref):
    out_ref[...] = value_ref[...].astype(F32).T


def same_body(value_ref, out_ref):
    out_ref[...] = value_ref[...]


def wide_body(value_ref, out_ref):
    out_ref[...] = value_ref[...].astype(F32)


def on_device(
    h_in,
    memory,
    cotangent,
    block_docs,
    w_query,
    w_out,
    self_key_value_weight,
    cache_key_value_weight,
):
    section_id = lax.axis_index("section")
    section_count = lax.axis_size("section")
    shard_id = lax.axis_index("seq")
    tp_id = lax.axis_index("tp")
    tp_count = lax.axis_size("tp")
    self_section = section_id == 0
    hidden = h_in[0]
    grad_local = cotangent[0]
    source = jnp.where(self_section, hidden, memory[0])

    def gathered(own):
        return [own] + [shifted(own, "tp", step) for step in range(1, tp_count)]

    source_pieces = gathered(source)
    hidden_pieces = gathered(hidden)
    grad_pieces = gathered(grad_local)

    rows, width = hidden.shape
    model = width * tp_count
    per = rows // BLK
    query_weight = w_query[0]
    out_weight = w_out[0]
    kv_weight = jnp.where(self_section, self_key_value_weight, cache_key_value_weight)
    kv_cols = self_key_value_weight.shape[2]
    kv_heads = kv_cols // HEAD_DIM
    query_cols = query_weight.shape[1]
    heads = query_cols // HEAD_DIM
    kv_flat = kv_weight.reshape(model, 2 * kv_cols)
    me = tp_id.astype(jnp.int32).reshape(1)

    all_docs = lax.all_gather(block_docs[0], "seq", axis=0, tiled=True)
    first_doc = lax.dynamic_slice_in_dim(all_docs, shard_id * per, 1)[0]
    first_block = jnp.sum((all_docs < first_doc).astype(jnp.int32)) // per
    window_block = jnp.maximum(shard_id * rows - WIN + 1, 0) // rows
    first_block = jnp.where(self_section, jnp.maximum(first_block, window_block), first_block)
    meta = jnp.concatenate(
        [
            jnp.stack([shard_id, self_section.astype(jnp.int32), first_block]).astype(jnp.int32),
            all_docs,
        ]
    )

    source_normed, source_factor, packed, key_raw = call(
        functools.partial(key_body, tp_count),
        [
            struct((rows, model), BF16),
            struct((rows, HEAD_DIM), F32),
            struct((rows, 2 * kv_cols), BF16),
            struct((rows, kv_cols), F32),
        ],
        [me, *source_pieces, kv_flat],
        1,
        2 * rows * model * 2 * kv_cols,
        limit=40,
        after=[meta],
    )
    all_kv = lax.all_gather(packed, "seq", axis=0, tiled=True)
    length = all_kv.shape[0]
    chips = length // rows // 2

    together = 2 if heads % 2 == 0 else 1
    whole = pl.BlockSpec((rows, width), lambda i: (0, 0))
    full = pl.BlockSpec((rows, model), lambda i: (0, 0))
    per_head = pl.BlockSpec((together, rows, HEAD_DIM), lambda i: (i, 0, 0))
    normed, row_factor, query_unit, query_raw = call(
        functools.partial(query_body, tp_count),
        [
            struct((rows, model), BF16),
            struct((rows, HEAD_DIM), F32),
            struct((heads, rows, HEAD_DIM), BF16),
            struct((heads, rows, HEAD_DIM), F32),
        ],
        [me, *hidden_pieces, query_weight],
        1,
        2 * rows * model * query_cols,
        after=[packed],
        grid=(heads // together,),
        in_specs=[SMEM]
        + [whole] * tp_count
        + [pl.BlockSpec((model, together * HEAD_DIM), lambda i: (0, i))],
        out_specs=[
            full,
            pl.BlockSpec((rows, HEAD_DIM), lambda i: (0, 0)),
            per_head,
            per_head,
        ],
    )
    attn_flat, log_denom = call(
        functools.partial(forward_body, kv_heads),
        [struct((rows, query_cols), BF16), struct((heads, rows, HEAD_DIM), F32)],
        [meta, query_unit, all_kv],
        1,
        4 * rows * length * query_cols,
        [pltpu.VMEM((heads, rows, HEAD_DIM), F32)] * 2,
    )
    out_share, mark = scattered(grad_pieces, attn_flat)
    (grad_attn,) = call(
        functools.partial(grad_attn_body, tp_count),
        [struct((heads, rows, HEAD_DIM), BF16)],
        [me, *grad_pieces, out_weight],
        1,
        2 * rows * model * query_cols,
        after=[mark],
        grid=(heads // together,),
        in_specs=[SMEM]
        + [whole] * tp_count
        + [pl.BlockSpec((together * HEAD_DIM, model), lambda i: (i, 0))],
        out_specs=[per_head],
    )
    halves = [struct((chips, rows, 2 * kv_cols), BF16)] + [
        struct((rows, 2 * kv_cols), BF16)
    ] * chips
    keep, *send, grad_queries = call(
        functools.partial(backward_body, kv_heads),
        halves + [struct((rows, query_cols), BF16)],
        [meta, query_unit, query_raw, grad_attn, attn_flat, log_denom, all_kv],
        1,
        10 * rows * length * query_cols,
        [pltpu.VMEM((heads, rows, HEAD_DIM), F32)] * 2,
        after=[mark],
    )
    kv_came = [core_swap(piece) for piece in send]
    query_keep, query_low, query_high, _ = over_tokens(normed, grad_queries, natural=True)
    kv_sums, mark, query_sum = sums_below(
        keep, kv_came, [query_keep, core_swap(query_low), core_swap(query_high)], []
    )
    query_share = lax.psum_scatter(
        query_sum.reshape(-1, query_cols),
        "seq",
        scatter_dimension=0,
        tiled=True,
        axis_index_groups=[[2 * one + core for one in range(chips)] for core in range(2)],
    )

    wide = struct((rows, width), BF16)
    broad = struct((rows, HEAD_DIM), F32)
    projected, *projected_sent = call(
        functools.partial(project_body, tp_count),
        split_shapes(rows, width, tp_count, False),
        [me, attn_flat, out_weight],
        1,
        2 * rows * model * query_cols,
        after=[mark],
    )
    rows_part, *rows_sent, row_dot = call(
        functools.partial(back_body, tp_count),
        split_shapes(rows, width, tp_count, True) + [broad],
        [me, grad_queries, query_weight, *hidden_pieces],
        1,
        2 * rows * model * query_cols,
        after=[projected],
    )
    (kv_grad,) = call(
        key_grad_body,
        [struct((rows, 2 * kv_cols), BF16)],
        [key_raw, *kv_sums],
        0,
        0,
        after=[row_dot],
        limit=16,
    )
    kv_keep, kv_low, kv_high, relayed = over_tokens(
        source_normed, kv_grad, (), [*rows_sent, *projected_sent]
    )
    others = tp_count - 1
    projected_came = sent_over_tp(relayed[others:])
    rows_came = sent_over_tp(relayed[:others])
    kv_sum = Halving(kv_keep, kv_low, kv_high)
    mark, _ = kv_sum.step([kv_keep])
    source_part, *source_sent, source_dot = call(
        functools.partial(back_body, tp_count),
        split_shapes(rows, width, tp_count, True) + [broad],
        [me, kv_grad, kv_flat, *source_pieces],
        1,
        4 * rows * model * kv_cols,
        after=[mark],
    )
    tile = pl.BlockSpec((rows, width), lambda i, at: (0, 0))
    h_out, *source_sent = ordered(
        output_body,
        [hidden, projected, *projected_came],
        [source_dot],
        [wide],
        (1,),
        [tile] * (2 + others),
        [tile],
        jnp.zeros((1,), jnp.int32),
        source_sent,
    )
    source_came = sent_over_tp(source_sent)
    passed_came = shifted(h_out, "section", 1)
    mark = h_out
    (out_grad,) = call(
        flip_body,
        [struct((query_cols, out_share.shape[0]), F32)],
        [out_share],
        0,
        0,
        after=[h_out],
    )
    (grad_input,) = call(
        functools.partial(input_body, True, model),
        [wide],
        [grad_local, hidden, row_factor, row_dot, rows_part, *rows_came],
        0,
        0,
        after=[out_grad],
    )
    mark = grad_input
    while kv_sum.count > 2:
        mark, _ = kv_sum.step([mark])
    kv_parts = kv_sum.finish([mark])
    (grad_memory,) = call(
        functools.partial(input_body, False, model),
        [wide],
        [source, source_factor, source_dot, source_part, *source_came],
        0,
        0,
        after=[kv_parts[0]],
    )
    (passed,) = call(same_body, [wide], [passed_came], 0, 0, after=[grad_memory])
    (query_grad,) = call(
        wide_body, [struct(query_share.shape, F32)], [query_share], 0, 0, after=[passed]
    )
    share_rows = kv_parts[0].shape[0]
    self_grad, cache_grad = call(
        functools.partial(section_body, section_count),
        [struct((share_rows, 2, kv_cols), F32)] * 2,
        [section_id.astype(jnp.int32).reshape(1), *kv_parts],
        1,
        0,
        after=[query_grad],
    )
    return (
        passed[None],
        grad_input[None],
        grad_memory[None],
        query_grad[None],
        out_grad[None],
        self_grad,
        cache_grad,
    )


def solution(mesh):
    return jax.shard_map(
        on_device,
        mesh=mesh,
        in_specs=(
            P("section", "seq", "tp"),
            P("section", "seq", "tp"),
            P("section", "seq", "tp"),
            P("section", "seq"),
            P("section", None, "tp"),
            P("section", "tp", None),
            P(None, None, "tp"),
            P(None, None, "tp"),
        ),
        out_specs=(
            P("section", "seq", "tp"),
            P("section", "seq", "tp"),
            P("section", "seq", "tp"),
            P("section", "seq", "tp"),
            P("section", "tp", "seq"),
            P(("seq", "section"), None, "tp"),
            P(("seq", "section"), None, "tp"),
        ),
        check_vma=False,
    )
```

```python
import functools
import math

import jax
import jax.numpy as jnp
from jax import lax
from jax.experimental import pallas as pl
from jax.experimental.pallas import tpu as pltpu
from jax.sharding import PartitionSpec as P

HEAD_DIM = 128
BLK = 128
WIN = 1024

score_scale = 40.0
norm_eps = 1e-06
log2_e = math.log2(math.e)

F32 = jnp.float32
BF16 = jnp.bfloat16
NN = (((1,), (0,)), ((), ()))
NT = (((1,), (1,)), ((), ()))
TN = (((0,), (0,)), ((), ()))

VMEM = pl.BlockSpec(memory_space=pltpu.VMEM)
SMEM = pl.BlockSpec(memory_space=pltpu.SMEM)


def dot(left, right, dims):
    return lax.dot_general(left, right, dims, preferred_element_type=F32)


def shifted(value, axis, steps):
    count = lax.axis_size(axis)
    pairs = [(source, (source + steps) % count) for source in range(count)]
    return lax.ppermute(value, axis, pairs)


def call(
    body, out_shape, inputs, smem_count, flops, scratch=(), limit=60, after=(),
    grid=(), in_specs=None, out_specs=None,
):
    moved = sum(v.size * v.dtype.itemsize for v in inputs) + sum(
        o.size * o.dtype.itemsize for o in out_shape
    )
    if in_specs is None:
        in_specs = [SMEM] * smem_count + [VMEM] * (len(inputs) - smem_count)
    if out_specs is None:
        out_specs = [VMEM] * len(out_shape)

    def with_order(*refs):
        body(*refs[: len(inputs)], *refs[len(inputs) + len(after) :])

    return pl.pallas_call(
        with_order,
        out_shape=out_shape,
        grid=grid,
        in_specs=list(in_specs) + [pl.BlockSpec(memory_space=pl.ANY)] * len(after),
        out_specs=out_specs,
        scratch_shapes=list(scratch),
        compiler_params=pltpu.CompilerParams(vmem_limit_bytes=limit * 1024 * 1024),
        cost_estimate=pl.CostEstimate(flops=flops, bytes_accessed=moved, transcendentals=0),
    )(*inputs, *after)


def struct(shape, dtype):
    return jax.ShapeDtypeStruct(shape, dtype)


def offset(me, count, step, width):
    return pl.multiple_of(lax.rem(me + count - step, count) * width, width)


def normalize(pieces, me, normed_ref, factor_ref):
    count = len(pieces)
    width = pieces[0].shape[1]
    total = 0.0
    for piece in pieces:
        wide = piece[...].astype(F32)
        total = total + jnp.sum(wide * wide, axis=1, keepdims=True)
    factor = lax.rsqrt(total / (count * width) + norm_eps)
    factor_ref[...] = jnp.broadcast_to(factor, factor_ref.shape)
    for step, piece in enumerate(pieces):
        normed_ref[:, pl.ds(offset(me, count, step, width), width)] = (
            piece[...].astype(F32) * factor
        ).astype(BF16)


def unit(raw):
    return raw * lax.rsqrt(jnp.sum(raw * raw, axis=1, keepdims=True) + norm_eps)


def unit_back(raw, grad):
    scale = lax.rsqrt(jnp.sum(raw * raw, axis=1, keepdims=True) + norm_eps)
    along = jnp.sum(raw * grad, axis=1, keepdims=True)
    return scale * grad - raw * (scale * scale * scale * along)


def query_body(count, me_ref, *refs):
    pieces, (weight, normed_ref, factor_ref, unit_ref, raw_ref) = refs[:count], refs[count:]

    @pl.when(pl.program_id(0) == 0)
    def first():
        normalize(pieces, me_ref[0], normed_ref, factor_ref)

    both = dot(normed_ref[...], weight[...], NN)
    for head in range(unit_ref.shape[0]):
        raw = both[:, head * HEAD_DIM : (head + 1) * HEAD_DIM]
        raw_ref[head] = raw
        unit_ref[head] = unit(raw).astype(BF16)


def key_body(count, me_ref, *refs):
    pieces, (weight, normed_ref, factor_ref, packed_ref, raw_ref) = refs[:count], refs[count:]
    normalize(pieces, me_ref[0], normed_ref, factor_ref)
    both = dot(normed_ref[...], weight[...], NN)
    half = both.shape[1] // 2
    for head in range(half // HEAD_DIM):
        cols = slice(head * HEAD_DIM, (head + 1) * HEAD_DIM)
        packed_ref[:, cols] = unit(both[:, cols]).astype(BF16)
    packed_ref[:, half:] = both[:, half:].astype(BF16)
    raw_ref[...] = both[:, :half]


def allowed_block(meta, block, rows):
    per = rows // BLK
    shard, self_section = meta[0], meta[1]
    shape = (rows, rows)
    query = lax.broadcasted_iota(jnp.int32, shape, 0)
    key = lax.broadcasted_iota(jnp.int32, shape, 1)
    query_doc = jnp.full(shape, meta[3 + shard * per], jnp.int32)
    key_doc = jnp.full(shape, meta[3 + block * per], jnp.int32)
    for part in range(1, per):
        query_doc = jnp.where(query >= part * BLK, meta[3 + shard * per + part], query_doc)
        key_doc = jnp.where(key >= part * BLK, meta[3 + block * per + part], key_doc)
    query_pos = shard * rows + query
    key_pos = block * rows + key
    is_self = jnp.full(shape, self_section, jnp.int32) == 1
    upper = jnp.where(is_self, query_pos, query_pos // BLK * BLK + BLK - 1)
    lower = jnp.where(is_self, query_pos - WIN, -1)
    return (query_doc == key_doc) & (key_pos <= upper) & (key_pos > lower)


def key_value(kv_ref, span, kv_head, kv_heads):
    first = (kv_heads + kv_head) * HEAD_DIM
    key = kv_ref[span, kv_head * HEAD_DIM : (kv_head + 1) * HEAD_DIM]
    return key, kv_ref[span, first : first + HEAD_DIM]


def forward_body(kv_heads, meta, query_ref, kv_ref, out_ref, log_ref, number_ref, denom_ref):
    heads, rows, _ = query_ref.shape
    group = heads // kv_heads
    stacked = (group * rows, HEAD_DIM)
    number_ref[...] = jnp.zeros_like(number_ref)
    denom_ref[...] = jnp.zeros_like(denom_ref)

    def step(block, carry):
        allowed = allowed_block(meta, block, rows)
        span = pl.ds(pl.multiple_of(block * rows, rows), rows)
        for kv_head in range(kv_heads):
            mine = slice(kv_head * group, (kv_head + 1) * group)
            key, value = key_value(kv_ref, span, kv_head, kv_heads)
            score = dot(query_ref[mine].reshape(stacked), key, NT).reshape(group, rows, rows)
            weight = jnp.where(allowed[None], jnp.exp2(score * (score_scale * log2_e)), 0.0)
            folded = weight[:, :, :HEAD_DIM]
            for first in range(HEAD_DIM, rows, HEAD_DIM):
                folded = folded + weight[:, :, first : first + HEAD_DIM]
            denom_ref[mine] += folded
            product = dot(weight.astype(BF16).reshape(group * rows, rows), value, NN)
            number_ref[mine] += product.reshape(group, rows, HEAD_DIM)
        return carry

    lax.fori_loop(meta[2], meta[0] + 1, step, 0)
    for head in range(heads):
        denom = jnp.sum(denom_ref[head], axis=1, keepdims=True)
        log_ref[head] = jnp.broadcast_to(jnp.log2(denom), (rows, HEAD_DIM))
        out_ref[:, head * HEAD_DIM : (head + 1) * HEAD_DIM] = (number_ref[head] / denom).astype(BF16)


def grad_attn_body(count, me_ref, *refs):
    pieces, (weight, grad_ref) = refs[:count], refs[count:]
    width = pieces[0].shape[1]
    both = 0.0
    for step, piece in enumerate(pieces):
        span = pl.ds(offset(me_ref[0], count, step, width), width)
        both = both + dot(piece[...], weight[:, span], NT)
    for head in range(grad_ref.shape[0]):
        grad_ref[head] = both[:, head * HEAD_DIM : (head + 1) * HEAD_DIM].astype(BF16)


def backward_body(
    kv_heads, meta, query_ref, raw_ref, grad_ref, out_ref, log_ref, kv_ref,
    keep_ref, *refs,
):
    *send_refs, queries_ref, running_ref, delta_ref = refs
    heads, rows, _ = query_ref.shape
    group = heads // kv_heads
    stacked = (group * rows, HEAD_DIM)
    running_ref[...] = jnp.zeros_like(running_ref)
    keep_ref[...] = jnp.zeros_like(keep_ref)
    for send_ref in send_refs:
        send_ref[...] = jnp.zeros_like(send_ref)
    for head in range(heads):
        cols = slice(head * HEAD_DIM, (head + 1) * HEAD_DIM)
        product = grad_ref[head].astype(F32) * out_ref[:, cols].astype(F32)
        delta_ref[head] = jnp.broadcast_to(jnp.sum(product, axis=1, keepdims=True), (rows, HEAD_DIM))

    def widened(ref, mine):
        return jnp.concatenate([ref[mine].reshape(stacked)] * (rows // HEAD_DIM), axis=1)

    def step(block, carry):
        allowed = allowed_block(meta, block, rows)
        span = pl.ds(pl.multiple_of(block * rows, rows), rows)
        for kv_head in range(kv_heads):
            mine = slice(kv_head * group, (kv_head + 1) * group)
            key, value = key_value(kv_ref, span, kv_head, kv_heads)
            query = query_ref[mine].reshape(stacked)
            grad = grad_ref[mine].reshape(stacked)
            score = dot(query, key, NT)
            probs = jnp.exp2(score * (score_scale * log2_e) - widened(log_ref, mine))
            probs = jnp.where(allowed[None], probs.reshape(group, rows, rows), 0.0)
            probs = probs.reshape(group * rows, rows)
            grad_probs = dot(grad, value, NT)
            grad_scores = (probs * (grad_probs - widened(delta_ref, mine))).astype(BF16)
            running_ref[mine] += dot(grad_scores, key, NN).reshape(group, rows, HEAD_DIM)
            key_term = (score_scale * dot(grad_scores, query, TN)).astype(BF16)
            value_term = dot(probs.astype(BF16), grad, TN).astype(BF16)
            low = kv_head * HEAD_DIM
            high = (kv_heads + kv_head) * HEAD_DIM

            steps = meta[0] // 2 - block // 2
            same_core = block % 2 == meta[0] % 2

            @pl.when(same_core)
            def own():
                keep_ref[steps, :, low : low + HEAD_DIM] = key_term
                keep_ref[steps, :, high : high + HEAD_DIM] = value_term

            for place, send_ref in enumerate(send_refs):

                def other(send_ref=send_ref):
                    send_ref[:, low : low + HEAD_DIM] = key_term
                    send_ref[:, high : high + HEAD_DIM] = value_term

                pl.when(jnp.logical_not(same_core) & (steps == place))(other)
        return carry

    lax.fori_loop(meta[2], meta[0] + 1, step, 0)
    for head in range(heads):
        queries_ref[:, head * HEAD_DIM : (head + 1) * HEAD_DIM] = unit_back(
            raw_ref[head], score_scale * running_ref[head]
        ).astype(BF16)


def split(count, transposed, me, left, weight_ref, pieces, outs, dot_ref):
    rows, width = outs[0].shape
    total = 0.0
    for step in list(range(1, count)) + [0]:
        span = pl.ds(offset(me, count, step, width), width)
        if transposed:
            part = dot(left, weight_ref[span, :], NT).astype(BF16)
        else:
            part = dot(left, weight_ref[:, span], NN).astype(BF16)
        outs[step][:, :width] = part
        if dot_ref is not None:
            total = total + jnp.sum(
                part.astype(F32) * pieces[step][...].astype(F32), axis=1, keepdims=True
            )
    if dot_ref is not None:
        dot_ref[...] = jnp.broadcast_to(total, dot_ref.shape)
        lane = lax.broadcasted_iota(jnp.int32, dot_ref.shape, 1)
        rest, column = total, jnp.zeros(dot_ref.shape, F32)
        for place in range(3):
            term = rest.astype(BF16).astype(F32)
            column = jnp.where(lane == place, term, column)
            rest = rest - term
        for out in outs[1:]:
            out[:, width:] = column.astype(BF16)


def split_shapes(rows, width, count, dotted):
    extra = HEAD_DIM if dotted else 0
    return [struct((rows, width), BF16)] + [struct((rows, width + extra), BF16)] * (count - 1)


def sent_over_tp(outs):
    return [shifted(out, "tp", -1 - index) for index, out in enumerate(outs)]


def project_body(count, me_ref, left_ref, weight_ref, *outs):
    split(count, False, me_ref[0], left_ref[...], weight_ref, None, outs, None)


def back_body(count, me_ref, left_ref, weight_ref, *refs):
    pieces, outs, dot_ref = refs[:count], refs[count:-1], refs[-1]
    split(count, True, me_ref[0], left_ref[...], weight_ref, pieces, outs, dot_ref)


def key_grad_body(raw_ref, *refs):
    term_refs, grad_ref = refs[:-1], refs[-1]
    half = raw_ref.shape[1]
    total = sum(term[...].astype(F32) for term in term_refs)
    for first in range(0, half, HEAD_DIM):
        cols = slice(first, first + HEAD_DIM)
        grad_ref[:, cols] = unit_back(raw_ref[:, cols], total[:, cols]).astype(BF16)
    grad_ref[:, half:] = total[:, half:].astype(BF16)


def output_body(at_ref, hidden_ref, own_ref, *refs):
    total = hidden_ref[...].astype(F32) + sum(ref[...].astype(F32) for ref in (own_ref, *refs[:-1]))
    refs[-1][...] = total.astype(BF16)


def input_body(residual, model, *refs):
    base, refs = (refs[0], refs[1:]) if residual else (None, refs)
    values_ref, factor_ref, dot_ref, own_ref, *came, out_ref = refs
    width = own_ref.shape[1]
    total = own_ref[...].astype(F32)
    dot_total = dot_ref[:, :1]
    for ref in came:
        total = total + ref[:, :width].astype(F32)
        column = ref[:, width:].astype(F32)
        dot_total = dot_total + (column[:, :1] + column[:, 1:2] + column[:, 2:3])
    factor = factor_ref[:, :1]
    grad = factor * total - values_ref[...].astype(F32) * (
        factor * factor * factor * dot_total / model
    )
    if residual:
        grad = grad + base[...].astype(F32)
    out_ref[...] = grad.astype(BF16)


def flipped_bits(value, count):
    out, left = 0, count
    while left > 1:
        out = out * 2 + value % 2
        value, left = value // 2, left // 2
    return out


def tokens_body(at_ref, left_ref, right_ref, keep_ref, *send_refs):
    both = dot(left_ref[...], right_ref[...], TN).astype(BF16)
    half = both.shape[0] // 2

    @pl.when(at_ref[0] == 0)
    def low():
        keep_ref[0] = both[:half]

    @pl.when(at_ref[0] == 1)
    def high():
        keep_ref[0] = both[half:]

    tall = send_refs[0].shape[0]
    place = pl.program_id(0)
    for group, send_ref in enumerate(send_refs):

        @pl.when((at_ref[0] == 0) & (place // tall == group))
        def low_sent(send_ref=send_ref):
            send_ref[place % tall] = both[half:]

        @pl.when((at_ref[0] == 1) & (place // tall == group))
        def high_sent(send_ref=send_ref):
            send_ref[place % tall] = both[:half]


def ordered(
    body, inputs, after, outs, grid, in_specs, out_specs, scalars, relay=(), scratch=()
):
    kept = 1 + len(inputs)
    first = kept + len(after)
    anywhere = pl.BlockSpec(memory_space=pl.ANY)

    def with_order(*refs):
        begin = first + len(relay)
        last = begin + len(outs)
        body(*refs[:kept], *refs[begin:last], *refs[last + len(relay) :])

    return pl.pallas_call(
        with_order,
        out_shape=outs + [struct(value.shape, value.dtype) for value in relay],
        grid_spec=pltpu.PrefetchScalarGridSpec(
            num_scalar_prefetch=1,
            grid=grid,
            in_specs=in_specs + [anywhere] * (len(after) + len(relay)),
            out_specs=out_specs + [anywhere] * len(relay),
            scratch_shapes=list(scratch),
        ),
        input_output_aliases={first + i: len(outs) + i for i in range(len(relay))},
        compiler_params=pltpu.CompilerParams(vmem_limit_bytes=16 * 1024 * 1024),
        cost_estimate=pl.CostEstimate(flops=0, bytes_accessed=1024, transcendentals=0),
    )(scalars, *inputs, *after, *relay)


def over_tokens(left, right, after=(), relay=(), natural=False):
    rows, model = left.shape
    chips = lax.axis_size("seq") // 2
    step = model // chips
    cols = right.shape[1]
    shard = lax.axis_index("seq").astype(jnp.int32)
    near = jnp.stack(
        [shard % 2]
        + [
            jnp.int32(i) if natural else lax.bitwise_xor(shard // 2, jnp.int32(flipped_bits(i, chips)))
            for i in range(chips)
        ]
    )
    share = (step // 2, cols)
    group = (chips // 2, *share)
    keep, low, high, *relayed = ordered(
        tokens_body,
        [left, right],
        after,
        [struct((chips, *share), BF16), struct(group, BF16), struct(group, BF16)],
        (chips,),
        [
            pl.BlockSpec((rows, step), lambda i, at: (0, at[1 + i])),
            pl.BlockSpec(right.shape, lambda i, at: (0, 0)),
        ],
        [pl.BlockSpec((1, *share), lambda i, at: (i, 0, 0))]
        + [pl.BlockSpec(group, lambda i, at: (0, 0, 0))] * 2,
        near,
        relay,
    )
    return keep, low, high, relayed


def add_body(at_ref, *refs):
    out_ref = refs[-1]
    for index in range(out_ref.shape[0]):
        total = sum(ref[index].astype(F32) for ref in refs[:-1])
        out_ref[index] = total.astype(out_ref.dtype)


def added(keep, came, terms, first, count, dtype, after, relay=()):
    rows, cols = keep.shape[1:]
    block = pl.BlockSpec((count, rows, cols), lambda i, at: (first // count, 0, 0))
    start = pl.BlockSpec((count, rows, cols), lambda i, at: (0, 0, 0))
    return ordered(
        add_body,
        [keep, came, *terms],
        after,
        [struct((count, rows, cols), dtype)],
        (1,),
        [block, start if came.shape[0] == count and first > 0 else block] + [block] * len(terms),
        [start],
        jnp.zeros((1,), jnp.int32),
        relay,
    )


def core_swap(value):
    count = lax.axis_size("seq")
    return lax.ppermute(value, "seq", [(shard, shard ^ 1) for shard in range(count)])


def whole_body(left_ref, right_ref, out_ref):
    out_ref[...] = dot(left_ref[...], right_ref[...], TN).astype(BF16)


def pieces_body(count, parts, at_ref, *refs):
    pieces, (right_ref, keep_ref, low_ref, high_ref, both_ref) = refs[:count], refs[count:]
    step = pl.program_id(0)
    for which, piece in enumerate(pieces):

        @pl.when(step // parts == which)
        def multiply(piece=piece):
            both_ref[...] = dot(piece[...], right_ref[...], TN).astype(BF16)

    half = both_ref.shape[0] // 2
    tall = low_ref.shape[0]
    place = at_ref[1 + step]
    for core in range(2):
        mine = slice(core * half, (core + 1) * half)
        other = slice((1 - core) * half, (2 - core) * half)

        @pl.when(at_ref[0] == core)
        def kept(mine=mine):
            keep_ref[0] = both_ref[mine]

        @pl.when((at_ref[0] == core) & (place < tall))
        def low_sent(other=other):
            low_ref[place % tall] = both_ref[other]

        @pl.when((at_ref[0] == core) & (place >= tall))
        def high_sent(other=other):
            high_ref[place % tall] = both_ref[other]


def core_sum_body(at_ref, keep_ref, low_ref, high_ref, out_ref):
    half = low_ref.shape[0]
    for index in range(2 * half):
        other = low_ref[index] if index < half else high_ref[index - half]
        out_ref[index] = (keep_ref[index].astype(F32) + other.astype(F32)).astype(BF16)


def piece_products(pieces, right):
    rows, width = pieces[0].shape
    count = len(pieces)
    chips = lax.axis_size("seq") // 2
    cols = right.shape[1]
    step = width * count // chips
    parts = width // step
    core = lax.axis_index("seq").astype(jnp.int32) % 2
    tp_id = lax.axis_index("tp").astype(jnp.int32)
    places = [
        lax.rem(tp_id + count - which, count) * parts + part
        for which in range(count)
        for part in range(parts)
    ]
    share = (step // 2, cols)
    group = (chips // 2, *share)

    def picked(which):
        def index(i, at):
            held = jnp.where(i // parts < which, 0, parts - 1)
            return 0, jnp.where(i // parts == which, i % parts, held)

        return pl.BlockSpec((rows, step), index)

    return ordered(
        functools.partial(pieces_body, count, parts),
        [*pieces, right],
        (),
        [struct((chips, *share), BF16), struct(group, BF16), struct(group, BF16)],
        (chips,),
        [picked(which) for which in range(count)]
        + [pl.BlockSpec(right.shape, lambda i, at: (0, 0))],
        [pl.BlockSpec((1, *share), lambda i, at: (at[1 + i], 0, 0))]
        + [pl.BlockSpec(group, lambda i, at: (0, 0, 0))] * 2,
        jnp.stack([core] + places).astype(jnp.int32),
        scratch=[pltpu.VMEM((step, cols), BF16)],
    )


def core_sum(keep, low, high, after):
    full = pl.BlockSpec(keep.shape, lambda i, at: (0, 0, 0))
    half = pl.BlockSpec(low.shape, lambda i, at: (0, 0, 0))
    (total,) = ordered(
        core_sum_body,
        [keep, core_swap(low), core_swap(high)],
        after,
        [struct(keep.shape, BF16)],
        (1,),
        [full, half, half],
        [full],
        jnp.zeros((1,), jnp.int32),
    )
    return total


def over_chips(total):
    chips = total.shape[0]
    groups = [[2 * one + core for one in range(chips)] for core in range(2)]
    flat = total.reshape(-1, total.shape[2])
    return lax.psum_scatter(
        flat, "seq", scatter_dimension=0, tiled=True, axis_index_groups=groups
    )


def chip_sum_body(count, keep_ref, *refs):
    came, refs = refs[:count], refs[count:]
    whole_ref, low_ref, high_ref, out_ref = *refs[:3], refs[3 + count]
    for index in range(count):
        total = keep_ref[index].astype(F32) + came[index][...].astype(F32)
        refs[3 + index][...] = total.astype(BF16)
    half = count // 2
    for index in range(count):
        other = low_ref[index] if index < half else high_ref[index - half]
        total = whole_ref[index].astype(F32) + other.astype(F32)
        out_ref[index] = total.astype(BF16)


def sums_below(keep, came, query, after):
    chips, rows, cols = keep.shape
    *sums, query_sum = call(
        functools.partial(chip_sum_body, chips),
        [struct((rows, cols), BF16)] * chips + [struct(query[0].shape, BF16)],
        [keep, *came, *query],
        0,
        2 * keep.size,
        after=after,
        limit=24,
    )
    terms = [sums[0]]
    for steps in range(1, chips):
        pairs = [(shard, shard - 2 * steps) for shard in range(2 * steps, 2 * chips)]
        terms.append(lax.ppermute(sums[steps], "seq", pairs))
    return terms, sums[0], query_sum


class Halving:
    def __init__(self, keep, low, high):
        self.keep = keep
        self.high, self.low = core_swap(high), core_swap(low)
        self.terms = []
        self.count = keep.shape[0]
        self.distance = 2

    def step(self, after, relay=()):
        self.count //= 2
        came = self.low if self.terms else self.high
        sent, *relayed = added(
            self.keep, came, self.terms, self.count, self.count, BF16, after, relay
        )
        pairs = [(shard, shard ^ self.distance) for shard in range(lax.axis_size("seq"))]
        self.terms.append(lax.ppermute(sent, "seq", pairs))
        self.distance *= 2
        return sent, relayed

    def finish(self, after):
        rows, cols = self.keep.shape[1:]
        sections = lax.axis_size("section")
        section = lax.axis_index("section")
        share = rows // sections
        piece = struct((share, cols), BF16)
        block = pl.BlockSpec((2, rows, cols), lambda i, at: (0, 0, 0))
        flat = pl.BlockSpec((share, cols), lambda i, at: (0, 0))
        targets = [lax.rem(section + step, sections) for step in range(sections)]
        outs = ordered(
            last_body,
            [self.keep, self.low, *self.terms],
            after,
            [piece] * (2 * sections),
            (1,),
            [block] * (2 + len(self.terms)),
            [flat] * (2 * sections),
            jnp.stack(targets).astype(jnp.int32),
            scratch=[pltpu.VMEM((2, rows, cols), F32)],
        )
        count = lax.axis_size("seq")
        parts = list(outs[:1])
        for step in range(sections):
            pairs = [
                (shard * sections + one, (shard ^ self.distance) * sections + (one + step) % sections)
                for shard in range(count)
                for one in range(sections)
            ]
            parts.append(lax.ppermute(outs[sections + step], ("seq", "section"), pairs))
            if step > 0:
                parts.append(shifted(outs[step], "section", step))
        return parts


def last_body(at_ref, *refs):
    sections = at_ref.shape[0]
    terms, outs, total_ref = refs[: -2 * sections - 1], refs[-2 * sections - 1 : -1], refs[-1]
    share = outs[0].shape[0]
    for place in range(2):
        total_ref[place] = sum(ref[place].astype(F32) for ref in terms)
        for step in range(sections):
            span = pl.ds(pl.multiple_of(at_ref[step] * share, share), share)
            outs[place * sections + step][...] = total_ref[place, span, :].astype(BF16)


def section_body(sections, section_ref, *refs):
    parts, (self_ref, cache_ref) = refs[:-2], refs[-2:]
    section = section_ref[0]
    groups = [[parts[0], parts[1]]] + [
        [parts[2 * step], parts[2 * step + 1]] for step in range(1, sections)
    ]
    own = jnp.zeros(parts[0].shape, F32)
    other = jnp.zeros(parts[0].shape, F32)
    for step, group in enumerate(groups):
        total = group[0][...].astype(F32) + group[1][...].astype(F32)
        from_self = jnp.full(total.shape, section, jnp.int32) == step
        own = own + jnp.where(from_self, total, 0.0)
        other = other + jnp.where(from_self, 0.0, total)
    half = own.shape[1] // 2
    for kind in range(2):
        self_ref[:, kind, :] = own[:, kind * half : (kind + 1) * half]
        cache_ref[:, kind, :] = other[:, kind * half : (kind + 1) * half]


def flip_body(value_ref, out_ref):
    out_ref[...] = value_ref[...].astype(F32).T


def same_body(value_ref, out_ref):
    out_ref[...] = value_ref[...]


def wide_body(value_ref, out_ref):
    out_ref[...] = value_ref[...].astype(F32)


def on_device(
    h_in,
    memory,
    cotangent,
    block_docs,
    w_query,
    w_out,
    self_key_value_weight,
    cache_key_value_weight,
):
    section_id = lax.axis_index("section")
    section_count = lax.axis_size("section")
    shard_id = lax.axis_index("seq")
    tp_id = lax.axis_index("tp")
    tp_count = lax.axis_size("tp")
    self_section = section_id == 0
    hidden = h_in[0]
    grad_local = cotangent[0]
    source = jnp.where(self_section, hidden, memory[0])

    def gathered(own):
        return [own] + [shifted(own, "tp", step) for step in range(1, tp_count)]

    source_pieces = gathered(source)
    hidden_pieces = gathered(hidden)
    grad_pieces = gathered(grad_local)

    rows, width = hidden.shape
    model = width * tp_count
    per = rows // BLK
    query_weight = w_query[0]
    out_weight = w_out[0]
    kv_weight = jnp.where(self_section, self_key_value_weight, cache_key_value_weight)
    kv_cols = self_key_value_weight.shape[2]
    kv_heads = kv_cols // HEAD_DIM
    query_cols = query_weight.shape[1]
    heads = query_cols // HEAD_DIM
    kv_flat = kv_weight.reshape(model, 2 * kv_cols)
    me = tp_id.astype(jnp.int32).reshape(1)

    all_docs = lax.all_gather(block_docs[0], "seq", axis=0, tiled=True)
    first_doc = lax.dynamic_slice_in_dim(all_docs, shard_id * per, 1)[0]
    first_block = jnp.sum((all_docs < first_doc).astype(jnp.int32)) // per
    window_block = jnp.maximum(shard_id * rows - WIN + 1, 0) // rows
    first_block = jnp.where(self_section, jnp.maximum(first_block, window_block), first_block)
    meta = jnp.concatenate(
        [
            jnp.stack([shard_id, self_section.astype(jnp.int32), first_block]).astype(jnp.int32),
            all_docs,
        ]
    )

    source_normed, source_factor, packed, key_raw = call(
        functools.partial(key_body, tp_count),
        [
            struct((rows, model), BF16),
            struct((rows, HEAD_DIM), F32),
            struct((rows, 2 * kv_cols), BF16),
            struct((rows, kv_cols), F32),
        ],
        [me, *source_pieces, kv_flat],
        1,
        2 * rows * model * 2 * kv_cols,
        limit=40,
        after=[meta],
    )
    all_kv = lax.all_gather(packed, "seq", axis=0, tiled=True)
    length = all_kv.shape[0]
    chips = length // rows // 2

    together = 2 if heads % 2 == 0 else 1
    whole = pl.BlockSpec((rows, width), lambda i: (0, 0))
    full = pl.BlockSpec((rows, model), lambda i: (0, 0))
    per_head = pl.BlockSpec((together, rows, HEAD_DIM), lambda i: (i, 0, 0))
    normed, row_factor, query_unit, query_raw = call(
        functools.partial(query_body, tp_count),
        [
            struct((rows, model), BF16),
            struct((rows, HEAD_DIM), F32),
            struct((heads, rows, HEAD_DIM), BF16),
            struct((heads, rows, HEAD_DIM), F32),
        ],
        [me, *hidden_pieces, query_weight],
        1,
        2 * rows * model * query_cols,
        after=[packed],
        grid=(heads // together,),
        in_specs=[SMEM]
        + [whole] * tp_count
        + [pl.BlockSpec((model, together * HEAD_DIM), lambda i: (0, i))],
        out_specs=[
            full,
            pl.BlockSpec((rows, HEAD_DIM), lambda i: (0, 0)),
            per_head,
            per_head,
        ],
    )
    attn_flat, log_denom = call(
        functools.partial(forward_body, kv_heads),
        [struct((rows, query_cols), BF16), struct((heads, rows, HEAD_DIM), F32)],
        [meta, query_unit, all_kv],
        1,
        4 * rows * length * query_cols,
        [pltpu.VMEM((heads, rows, HEAD_DIM), F32)] * 2,
    )
    out_keep, out_low, out_high = piece_products(grad_pieces, attn_flat)
    (grad_attn,) = call(
        functools.partial(grad_attn_body, tp_count),
        [struct((heads, rows, HEAD_DIM), BF16)],
        [me, *grad_pieces, out_weight],
        1,
        2 * rows * model * query_cols,
        after=[out_keep],
        grid=(heads // together,),
        in_specs=[SMEM]
        + [whole] * tp_count
        + [pl.BlockSpec((together * HEAD_DIM, model), lambda i: (i, 0))],
        out_specs=[per_head],
    )
    out_total = core_sum(out_keep, out_low, out_high, [grad_attn])
    out_share = over_chips(out_total)
    halves = [struct((chips, rows, 2 * kv_cols), BF16)] + [
        struct((rows, 2 * kv_cols), BF16)
    ] * chips
    keep, *send, grad_queries = call(
        functools.partial(backward_body, kv_heads),
        halves + [struct((rows, query_cols), BF16)],
        [meta, query_unit, query_raw, grad_attn, attn_flat, log_denom, all_kv],
        1,
        10 * rows * length * query_cols,
        [pltpu.VMEM((heads, rows, HEAD_DIM), F32)] * 2,
        after=[out_total],
    )
    kv_came = [core_swap(piece) for piece in send]
    query_keep, query_low, query_high, _ = over_tokens(normed, grad_queries, natural=True)
    kv_sums, mark, query_sum = sums_below(
        keep, kv_came, [query_keep, core_swap(query_low), core_swap(query_high)], []
    )
    query_share = lax.psum_scatter(
        query_sum.reshape(-1, query_cols),
        "seq",
        scatter_dimension=0,
        tiled=True,
        axis_index_groups=[[2 * one + core for one in range(chips)] for core in range(2)],
    )

    wide = struct((rows, width), BF16)
    broad = struct((rows, HEAD_DIM), F32)
    projected, *projected_sent = call(
        functools.partial(project_body, tp_count),
        split_shapes(rows, width, tp_count, False),
        [me, attn_flat, out_weight],
        1,
        2 * rows * model * query_cols,
        after=[mark],
    )
    rows_part, *rows_sent, row_dot = call(
        functools.partial(back_body, tp_count),
        split_shapes(rows, width, tp_count, True) + [broad],
        [me, grad_queries, query_weight, *hidden_pieces],
        1,
        2 * rows * model * query_cols,
        after=[projected],
    )
    (kv_grad,) = call(
        key_grad_body,
        [struct((rows, 2 * kv_cols), BF16)],
        [key_raw, *kv_sums],
        0,
        0,
        after=[row_dot],
        limit=16,
    )
    kv_keep, kv_low, kv_high, relayed = over_tokens(
        source_normed, kv_grad, (), [*rows_sent, *projected_sent]
    )
    others = tp_count - 1
    projected_came = sent_over_tp(relayed[others:])
    rows_came = sent_over_tp(relayed[:others])
    kv_sum = Halving(kv_keep, kv_low, kv_high)
    mark, _ = kv_sum.step([kv_keep])
    source_part, *source_sent, source_dot = call(
        functools.partial(back_body, tp_count),
        split_shapes(rows, width, tp_count, True) + [broad],
        [me, kv_grad, kv_flat, *source_pieces],
        1,
        4 * rows * model * kv_cols,
        after=[mark],
    )
    tile = pl.BlockSpec((rows, width), lambda i, at: (0, 0))
    h_out, *source_sent = ordered(
        output_body,
        [hidden, projected, *projected_came],
        [source_dot],
        [wide],
        (1,),
        [tile] * (2 + others),
        [tile],
        jnp.zeros((1,), jnp.int32),
        source_sent,
    )
    source_came = sent_over_tp(source_sent)
    passed_came = shifted(h_out, "section", 1)
    mark = h_out
    (out_grad,) = call(
        flip_body,
        [struct((query_cols, out_share.shape[0]), F32)],
        [out_share],
        0,
        0,
        after=[h_out],
    )
    (grad_input,) = call(
        functools.partial(input_body, True, model),
        [wide],
        [grad_local, hidden, row_factor, row_dot, rows_part, *rows_came],
        0,
        0,
        after=[out_grad],
    )
    mark = grad_input
    while kv_sum.count > 2:
        mark, _ = kv_sum.step([mark])
    kv_parts = kv_sum.finish([mark])
    (grad_memory,) = call(
        functools.partial(input_body, False, model),
        [wide],
        [source, source_factor, source_dot, source_part, *source_came],
        0,
        0,
        after=[kv_parts[0]],
    )
    (passed,) = call(same_body, [wide], [passed_came], 0, 0, after=[grad_memory])
    (query_grad,) = call(
        wide_body, [struct(query_share.shape, F32)], [query_share], 0, 0, after=[passed]
    )
    share_rows = kv_parts[0].shape[0]
    self_grad, cache_grad = call(
        functools.partial(section_body, section_count),
        [struct((share_rows, 2, kv_cols), F32)] * 2,
        [section_id.astype(jnp.int32).reshape(1), *kv_parts],
        1,
        0,
        after=[query_grad],
    )
    return (
        passed[None],
        grad_input[None],
        grad_memory[None],
        query_grad[None],
        out_grad[None],
        self_grad,
        cache_grad,
    )


def solution(mesh):
    return jax.shard_map(
        on_device,
        mesh=mesh,
        in_specs=(
            P("section", "seq", "tp"),
            P("section", "seq", "tp"),
            P("section", "seq", "tp"),
            P("section", "seq"),
            P("section", None, "tp"),
            P("section", "tp", None),
            P(None, None, "tp"),
            P(None, None, "tp"),
        ),
        out_specs=(
            P("section", "seq", "tp"),
            P("section", "seq", "tp"),
            P("section", "seq", "tp"),
            P("section", "seq", "tp"),
            P("section", "tp", "seq"),
            P(("seq", "section"), None, "tp"),
            P(("seq", "section"), None, "tp"),
        ),
        check_vma=False,
    )
```
